512 devices in a mesh: head: 8 (over y), inner: 4 (over z_lo, core), outer: 16 (over z_hi, x).
Axes of the slice: x: 4, y: 8, z: 8 (z_hi: 4, z_lo: 2; z = z_hi * 2 + z_lo), core: 2. Of those that a mesh axis runs over, the one named last changes fastest.
Arguments:
- q_rows: bfloat16 [8192, 4096], P(('inner', 'outer', 'head')), may hold values from -8 to 8
- k_rows: bfloat16 [8192, 1024], P(('inner', 'outer', 'head')), may hold values from -8 to 8
- v_rows: bfloat16 [8192, 1024], P(('inner', 'outer', 'head')), may hold values from -6 to 6
- dout: bfloat16 [8192, 4096], P(('inner', 'outer'), 'head'), may hold values from -6 to 6
- positions: int32 [8192], replicated, may hold values from 0 to 8191, as said below
Outputs:
- attn_out: bfloat16 [8192, 4096], P(('inner', 'outer'), 'head')
- grad_q: bfloat16 [8192, 4096], P(('inner', 'outer'), 'head')
- grad_k: bfloat16 [8192, 1024], P(('inner', 'outer'), 'head')
- grad_v: bfloat16 [8192, 1024], P(('inner', 'outer'), 'head')
The draws below stay inside these ranges and needn't reach their ends.
Inputs may be any that keep to these rules, and one draw needn't show every extreme that they name: A permutation of the positions. The rows of block b (rows b*128 to (b+1)*128 - 1) hold, in rising order, the positions p*128/2 to (p+1)*128/2-1 in their first half and (127-p)*128/2 onward in their second half, for a p below 64 that differs from block to block.
All inputs are finite; a program needn't handle non-finite values.
Results may differ from the reference program's by a relative error of at most 0.012.
Values may be sent and summed in bfloat16 or wider, within the bound.
A program may use at most 64 MiB of HBM per device.

```python
import jax
import jax.numpy as jnp
from jax import lax

QH = 32
KVH = 8
DH = 128
TOK_DEV = 128
BLOCKS = 64
SEQ = 8192


def draw_q_rows(key, part):
    key = jax.random.fold_in(key, 3)
    result = jax.random.truncated_normal(key, -8.0, 8.0, (SEQ, QH, DH), jnp.float32)
    return result.reshape(SEQ, QH * DH).astype(jnp.bfloat16)


def draw_k_rows(key, part):
    key = jax.random.fold_in(key, 7)
    result = jax.random.truncated_normal(key, -8.0, 8.0, (SEQ, KVH, DH), jnp.float32)
    return result.reshape(SEQ, KVH * DH).astype(jnp.bfloat16)


def draw_positions(key, part):
    key = jax.random.fold_in(key, 5)
    order = jax.random.permutation(key, BLOCKS).astype(jnp.int32)
    rows = jnp.arange(SEQ, dtype=jnp.int32)
    block_of_row = rows // TOK_DEV
    row_in_block = rows % TOK_DEV
    half_rows = TOK_DEV // 2
    paired = order[block_of_row]
    first_run = paired * half_rows + row_in_block
    second_run = (2 * BLOCKS - 1 - paired) * half_rows + (row_in_block - half_rows)
    return jnp.where(row_in_block < half_rows, first_run, second_run).astype(jnp.int32)


def levels(rng, dims, cuts, least, high):
    level = 1.0
    for position, parts in cuts:
        draws = jax.random.uniform(jax.random.fold_in(jax.random.fold_in(rng, 6), position), (parts,), jnp.float32, least / len(cuts), high / len(cuts))
        level = level * jnp.repeat(jnp.exp(draws), dims[position] // parts).reshape((-1,) + (1,) * (len(dims) - 1 - position))
    return level


def noise(stream_key, shape, spread, bound, shards=(), kind=jnp.bfloat16):
    values = jax.random.normal(stream_key, shape, jnp.float32) * spread
    if len(shards) > 0:
        values = levels(stream_key, shape, shards, -0.22, 0.18) * values
    return jnp.clip(values, min=-bound, max=bound).astype(kind)


def setup_inputs(seed: int = 0) -> dict:
    key_list = jax.random.split(jax.random.key(seed), 6)
    return {
        "q_rows": draw_q_rows(jax.random.fold_in(key_list[5], 71), 0),
        "k_rows": draw_k_rows(jax.random.fold_in(key_list[5], 71), 0),
        "v_rows": noise(key_list[2], (SEQ, KVH * DH), 1.0, 6.0, ((0, 512),)),
        "dout": noise(key_list[3], (SEQ, QH * DH), 1.0, 6.0, ((0, 64), (1, 8))),
        "positions": draw_positions(jax.random.fold_in(key_list[5], 71), 0),
    }


def reference(q_rows, k_rows, v_rows, dout, positions):
    head_ratio = QH // KVH
    score_scale = DH ** -0.5
    visible = positions[None, :] <= positions[:, None]

    def per_head(head):
        group = head // head_ratio
        query_head = lax.dynamic_slice_in_dim(q_rows, head * DH, DH, 1)
        key_head = lax.dynamic_slice_in_dim(k_rows, group * DH, DH, 1)
        value_head = lax.dynamic_slice_in_dim(v_rows, group * DH, DH, 1)
        grad_head = lax.dynamic_slice_in_dim(dout, head * DH, DH, 1)
        scores = jnp.dot(query_head, key_head.T, preferred_element_type=jnp.float32) * score_scale
        log_sums = jax.nn.logsumexp(jnp.where(visible, scores, -jnp.inf), axis=1)
        clipped = jnp.where(visible, scores, log_sums[:, None])
        weights = jnp.where(visible, jnp.exp(clipped - log_sums[:, None]), 0.0)
        attn_head = jnp.dot(weights, value_head.astype(jnp.float32), precision=lax.Precision.HIGHEST).astype(jnp.bfloat16)
        attn_head = lax.optimization_barrier(attn_head)
        delta = jnp.sum(grad_head.astype(jnp.float32) * attn_head.astype(jnp.float32), axis=1)
        prob_rounded = lax.optimization_barrier(weights.astype(jnp.bfloat16))
        dprobs = jnp.dot(grad_head, value_head.T, preferred_element_type=jnp.float32)
        dscores = (prob_rounded.astype(jnp.float32) * (dprobs - delta[:, None]) * score_scale).astype(jnp.bfloat16)
        grad_query = jnp.dot(dscores, key_head, preferred_element_type=jnp.float32).astype(jnp.bfloat16)
        grad_key = jnp.dot(dscores.T, query_head, preferred_element_type=jnp.float32)
        grad_value = jnp.dot(prob_rounded.T, grad_head, preferred_element_type=jnp.float32)
        return attn_head, grad_query, grad_key, grad_value

    attn_all, gq_all, gk_all, gv_all = lax.map(per_head, jnp.arange(QH, dtype=jnp.int32))
    attn_out = jnp.transpose(attn_all, (1, 0, 2)).reshape(SEQ, QH * DH)
    grad_q = jnp.transpose(gq_all, (1, 0, 2)).reshape(SEQ, QH * DH)
    grad_k = jnp.transpose(gk_all.reshape(KVH, head_ratio, SEQ, DH).sum(axis=1), (1, 0, 2)).reshape(SEQ, KVH * DH)
    grad_v = jnp.transpose(gv_all.reshape(KVH, head_ratio, SEQ, DH).sum(axis=1), (1, 0, 2)).reshape(SEQ, KVH * DH)
    return attn_out, grad_q, grad_k.astype(jnp.bfloat16), grad_v.astype(jnp.bfloat16)
```

```python
import jax
import jax.numpy as jnp
from jax import lax
from jax.experimental import pallas as pl
from jax.experimental.pallas import tpu as pltpu
from jax.sharding import PartitionSpec as P

QH = 32
KVH = 8
DH = 128
RUN = 64
BLOCKS = 64
RATIO = QH // KVH
ROWS = RATIO * RUN
CHUNK = 256
RUNS_CHUNK = CHUNK // RUN
CHUNKS = 2 * BLOCKS // RUNS_CHUNK
ITEMS = CHUNKS + 1
LOG2E = 1.4426950408889634
SCALE = DH**-0.5
NEG_FILL = -1e30
F32 = jnp.float32
BF16 = jnp.bfloat16


def dot(a, b, ca, cb):
    return lax.dot_general(a, b, (((ca,), (cb,)), ((), ())), preferred_element_type=F32)


def attention_kernel(
    own_ref,
    pb_ref,
    q_ref,
    do_ref,
    kv_ref,
    out_ref,
    dq_ref,
    dkv_ref,
    loc,
    qs,
    dos,
    kvs,
    kvt,
    scores,
    probs,
    dkvs,
    top,
    total,
    acc_out,
    acc_dq,
    qd,
    dod,
    delta,
):
    own = pb_ref[own_ref[0]]
    first_chunks = own // RUNS_CHUNK

    def place(b, carry):
        p = pb_ref[b]
        loc[p] = 2 * b
        loc[2 * BLOCKS - 1 - p] = 2 * b + 1
        return carry

    lax.fori_loop(0, BLOCKS, place, 0)

    for s in range(2):
        rows = slice(s * RUN, (s + 1) * RUN)
        for h in range(RATIO):
            cols = slice(h * DH, (h + 1) * DH)
            qs[s, h * RUN : (h + 1) * RUN, :] = q_ref[rows, cols]
            dos[s, h * RUN : (h + 1) * RUN, :] = do_ref[rows, cols]

    def sort_chunk(c, carry):
        for j in range(RUNS_CHUNK):
            start = pl.multiple_of(loc[c * RUNS_CHUNK + j] * RUN, RUN)
            kvs[c, j * RUN : (j + 1) * RUN, :] = kv_ref[pl.ds(start, RUN), :]
        kvt[c] = kvs[c].T
        dkvs[c] = jnp.zeros((CHUNK, 2 * DH), F32)
        return carry

    lax.fori_loop(0, CHUNKS, sort_chunk, 0)

    top[...] = jnp.full(top.shape, NEG_FILL, F32)
    total[...] = jnp.zeros(total.shape, F32)
    acc_out[...] = jnp.zeros(acc_out.shape, F32)
    acc_dq[...] = jnp.zeros(acc_dq.shape, F32)

    def item(t):
        late = t >= first_chunks
        sel = jnp.where(late, 1, 0)
        return sel, jnp.where(late, t - first_chunks, t)

    def sweep(visit):
        def some(i, carry):
            for j in range(3):
                t = 3 * i + j
                sel, c = item(t)
                visit(t, sel, c, None)
            return carry

        lax.fori_loop(0, (ITEMS - 3) // 3, some, 0)
        sel, c = item(ITEMS - 3)
        visit(ITEMS - 3, sel, c, None)
        visit(ITEMS - 2, 0, first_chunks, own * RUN)
        visit(ITEMS - 1, 1, CHUNKS - 1 - first_chunks, (2 * BLOCKS - 1 - own) * RUN)

    def fold(x, op):
        return op(x.reshape(CHUNK // 8, 8, ROWS), axis=0)

    def score(t, sel, c, first_pos):
        s = dot(kvs[c, :, :DH], qs[sel], 1, 1)
        if first_pos is not None:
            key = c * CHUNK + lax.broadcasted_iota(jnp.int32, (CHUNK, ROWS), 0)
            row = first_pos + lax.rem(lax.broadcasted_iota(jnp.int32, (CHUNK, ROWS), 1), RUN)
            s = jnp.where(key <= row, s, NEG_FILL)
        scores[t] = s
        top[sel] = jnp.maximum(top[sel], fold(s, jnp.max))

    sweep(score)
    for s in range(2):
        m = jnp.max(top[s], axis=0, keepdims=True) * (SCALE * LOG2E)
        top[s] = jnp.broadcast_to(m, (8, ROWS))

    def weigh(t, sel, c, first_pos):
        e = jnp.exp2(scores[t] * (SCALE * LOG2E) - top[sel, 0:1, :])
        total[sel] += fold(e, jnp.sum)
        e = e.astype(BF16)
        probs[t] = e
        acc_out[sel] += dot(kvt[c, DH:, :], e, 1, 0)

    sweep(weigh)
    for s in range(2):
        inv = 1.0 / jnp.sum(total[s], axis=0, keepdims=True)
        out = (acc_out[s] * inv).astype(BF16).astype(F32)
        d_rows = dos[s].astype(F32)
        delta[s] = jnp.broadcast_to(jnp.sum(out * d_rows.T, axis=0, keepdims=True), (8, ROWS))
        total[s] = jnp.broadcast_to(inv, (8, ROWS))
        inv_rows = jnp.broadcast_to(inv, (DH, ROWS)).T
        dod[s] = (d_rows * inv_rows).astype(BF16)
        qd[s] = (qs[s].astype(F32) * (inv_rows * SCALE)).astype(BF16)
        out = out.T.astype(BF16)
        for h in range(RATIO):
            out_ref[s * RUN : (s + 1) * RUN, h * DH : (h + 1) * DH] = out[h * RUN : (h + 1) * RUN]

    def backward(t, sel, c, first_pos):
        e = probs[t]
        dp = dot(kvs[c, :, DH:], dos[sel], 1, 1)
        ds = (e.astype(F32) * (dp - delta[sel, 0:1, :])).astype(BF16)
        dkvs[c, :, DH:] += dot(e, dod[sel], 1, 0)
        dkvs[c, :, :DH] += dot(ds, qd[sel], 1, 0)
        acc_dq[sel] += dot(kvt[c, :DH, :], ds, 1, 0)

    sweep(backward)
    for s in range(2):
        grad = (acc_dq[s] * (total[s, 0:1, :] * SCALE)).T.astype(BF16)
        for h in range(RATIO):
            dq_ref[s * RUN : (s + 1) * RUN, h * DH : (h + 1) * DH] = grad[h * RUN : (h + 1) * RUN]

    def unsort_chunk(c, carry):
        for j in range(RUNS_CHUNK):
            start = pl.multiple_of(loc[c * RUNS_CHUNK + j] * RUN, RUN)
            dkv_ref[pl.ds(start, RUN), :] = dkvs[c, j * RUN : (j + 1) * RUN, :].astype(BF16)
        return carry

    lax.fori_loop(0, CHUNKS, unsort_chunk, 0)


def attention(own, pb, q, do, kv):
    rows, width = q.shape
    vmem = pl.BlockSpec(memory_space=pltpu.VMEM)
    smem = pl.BlockSpec(memory_space=pltpu.SMEM)
    return pl.pallas_call(
        attention_kernel,
        out_shape=(
            jax.ShapeDtypeStruct((rows, width), BF16),
            jax.ShapeDtypeStruct((rows, width), BF16),
            jax.ShapeDtypeStruct(kv.shape, BF16),
        ),
        in_specs=[smem, smem, vmem, vmem, vmem],
        out_specs=(vmem, vmem, vmem),
        scratch_shapes=[
            pltpu.SMEM((2 * BLOCKS,), jnp.int32),
            pltpu.VMEM((2, ROWS, DH), BF16),
            pltpu.VMEM((2, ROWS, DH), BF16),
            pltpu.VMEM((CHUNKS, CHUNK, 2 * DH), BF16),
            pltpu.VMEM((CHUNKS, 2 * DH, CHUNK), BF16),
            pltpu.VMEM((ITEMS, CHUNK, ROWS), F32),
            pltpu.VMEM((ITEMS, CHUNK, ROWS), BF16),
            pltpu.VMEM((CHUNKS, CHUNK, 2 * DH), F32),
            pltpu.VMEM((2, 8, ROWS), F32),
            pltpu.VMEM((2, 8, ROWS), F32),
            pltpu.VMEM((2, DH, ROWS), F32),
            pltpu.VMEM((2, DH, ROWS), F32),
            pltpu.VMEM((2, ROWS, DH), BF16),
            pltpu.VMEM((2, ROWS, DH), BF16),
            pltpu.VMEM((2, 8, ROWS), F32),
        ],
        compiler_params=pltpu.CompilerParams(vmem_limit_bytes=56 * 1024 * 1024),
    )(own, pb, q, do, kv)


def shards(q_rows, k_rows, v_rows, dout, positions):
    heads = lax.axis_size("head")
    tokens = q_rows.shape[0]
    q_width = q_rows.shape[1] // heads
    kv_width = k_rows.shape[1] // heads
    mixed = jnp.concatenate(
        [
            q_rows.reshape(tokens, heads, q_width),
            k_rows.reshape(tokens, heads, kv_width),
            v_rows.reshape(tokens, heads, kv_width),
        ],
        axis=2,
    )
    mine = lax.all_to_all(mixed, "head", split_axis=1, concat_axis=0, tiled=True)
    mine = mine.reshape(heads * tokens, q_width + 2 * kv_width)
    kv = lax.all_gather(mine[:, q_width:], ("inner", "outer"), axis=0, tiled=True)
    own = lax.axis_index("inner") * lax.axis_size("outer") + lax.axis_index("outer")
    pb = positions[:: 2 * RUN] // RUN
    attn_out, grad_q, dkv = attention(own.reshape(1), pb, mine[:, :q_width], dout, kv)
    dkv = lax.psum_scatter(dkv, ("inner", "outer"), scatter_dimension=0, tiled=True)
    return attn_out, grad_q, dkv[:, :kv_width], dkv[:, kv_width:]


def solution(mesh):
    return jax.shard_map(
        shards,
        mesh=mesh,
        in_specs=(
            P(("inner", "outer", "head"), None),
            P(("inner", "outer", "head"), None),
            P(("inner", "outer", "head"), None),
            P(("inner", "outer"), "head"),
            P(),
        ),
        out_specs=(
            P(("inner", "outer"), "head"),
            P(("inner", "outer"), "head"),
            P(("inner", "outer"), "head"),
            P(("inner", "outer"), "head"),
        ),
        check_vma=False,
    )
```

```python
import functools

import jax
import jax.numpy as jnp
from jax import lax
from jax.experimental import pallas as pl
from jax.experimental.pallas import tpu as pltpu
from jax.sharding import PartitionSpec as P

QH = 32
KVH = 8
DH = 128
RUN = 64
BLOCKS = 64
CHIPS_X = 4
RATIO = QH // KVH
ROWS = RATIO * RUN
CHUNK = 256
RUNS_CHUNK = CHUNK // RUN
CHUNKS = 2 * BLOCKS // RUNS_CHUNK
ITEMS = CHUNKS + 1
LOG2E = 1.4426950408889634
SCALE = DH**-0.5
NEG_FILL = -1e30
F32 = jnp.float32
BF16 = jnp.bfloat16


def dot(a, b, ca, cb):
    return lax.dot_general(a, b, (((ca,), (cb,)), ((), ())), preferred_element_type=F32)


def attention_kernel(
    own_ref,
    pb_ref,
    q_ref,
    do_ref,
    kv_ref,
    out_ref,
    dq_ref,
    dkv_ref,
    loc,
    qs,
    dos,
    kvs,
    kvt,
    scores,
    probs,
    dkvs,
    top,
    total,
    acc_out,
    acc_dq,
    qd,
    dod,
    delta,
):
    own = pb_ref[own_ref[0]]
    first_chunks = own // RUNS_CHUNK

    def place(b, carry):
        p = pb_ref[b]
        loc[p] = 2 * b
        loc[2 * BLOCKS - 1 - p] = 2 * b + 1
        return carry

    lax.fori_loop(0, BLOCKS, place, 0)

    for s in range(2):
        rows = slice(s * RUN, (s + 1) * RUN)
        for h in range(RATIO):
            cols = slice(h * DH, (h + 1) * DH)
            qs[s, h * RUN : (h + 1) * RUN, :] = q_ref[rows, cols]
            dos[s, h * RUN : (h + 1) * RUN, :] = do_ref[rows, cols]

    def sort_chunk(c, carry):
        for j in range(RUNS_CHUNK):
            start = pl.multiple_of(loc[c * RUNS_CHUNK + j] * RUN, RUN)
            kvs[c, j * RUN : (j + 1) * RUN, :] = kv_ref[pl.ds(start, RUN), :]
        kvt[c] = kvs[c].T
        dkvs[c] = jnp.zeros((CHUNK, 2 * DH), F32)
        return carry

    lax.fori_loop(0, CHUNKS, sort_chunk, 0)

    top[...] = jnp.full(top.shape, NEG_FILL, F32)
    total[...] = jnp.zeros(total.shape, F32)
    acc_out[...] = jnp.zeros(acc_out.shape, F32)
    acc_dq[...] = jnp.zeros(acc_dq.shape, F32)

    def item(t):
        late = t >= first_chunks
        sel = jnp.where(late, 1, 0)
        return sel, jnp.where(late, t - first_chunks, t)

    def sweep(visit):
        def some(i, carry):
            for j in range(3):
                t = 3 * i + j
                sel, c = item(t)
                visit(t, sel, c, None)
            return carry

        lax.fori_loop(0, (ITEMS - 3) // 3, some, 0)
        sel, c = item(ITEMS - 3)
        visit(ITEMS - 3, sel, c, None)
        visit(ITEMS - 2, 0, first_chunks, own * RUN)
        visit(ITEMS - 1, 1, CHUNKS - 1 - first_chunks, (2 * BLOCKS - 1 - own) * RUN)

    def fold(x, op):
        return op(x.reshape(CHUNK // 8, 8, ROWS), axis=0)

    def score(t, sel, c, first_pos):
        s = dot(kvs[c, :, :DH], qs[sel], 1, 1)
        if first_pos is not None:
            key = c * CHUNK + lax.broadcasted_iota(jnp.int32, (CHUNK, ROWS), 0)
            row = first_pos + lax.rem(lax.broadcasted_iota(jnp.int32, (CHUNK, ROWS), 1), RUN)
            s = jnp.where(key <= row, s, NEG_FILL)
        scores[t] = s
        top[sel] = jnp.maximum(top[sel], fold(s, jnp.max))

    sweep(score)
    for s in range(2):
        m = jnp.max(top[s], axis=0, keepdims=True) * (SCALE * LOG2E)
        top[s] = jnp.broadcast_to(m, (8, ROWS))

    def weigh(t, sel, c, first_pos):
        e = jnp.exp2(scores[t] * (SCALE * LOG2E) - top[sel, 0:1, :])
        total[sel] += fold(e, jnp.sum)
        e = e.astype(BF16)
        probs[t] = e
        acc_out[sel] += dot(kvt[c, DH:, :], e, 1, 0)

    sweep(weigh)
    for s in range(2):
        inv = 1.0 / jnp.sum(total[s], axis=0, keepdims=True)
        out = (acc_out[s] * inv).astype(BF16).astype(F32)
        d_rows = dos[s].astype(F32)
        delta[s] = jnp.broadcast_to(jnp.sum(out * d_rows.T, axis=0, keepdims=True), (8, ROWS))
        total[s] = jnp.broadcast_to(inv, (8, ROWS))
        inv_rows = jnp.broadcast_to(inv, (DH, ROWS)).T
        dod[s] = (d_rows * inv_rows).astype(BF16)
        qd[s] = (qs[s].astype(F32) * (inv_rows * SCALE)).astype(BF16)
        out = out.T.astype(BF16)
        for h in range(RATIO):
            out_ref[s * RUN : (s + 1) * RUN, h * DH : (h + 1) * DH] = out[h * RUN : (h + 1) * RUN]

    def backward(t, sel, c, first_pos):
        e = probs[t]
        dp = dot(kvs[c, :, DH:], dos[sel], 1, 1)
        ds = (e.astype(F32) * (dp - delta[sel, 0:1, :])).astype(BF16)
        dkvs[c, :, DH:] += dot(e, dod[sel], 1, 0)
        dkvs[c, :, :DH] += dot(ds, qd[sel], 1, 0)
        acc_dq[sel] += dot(kvt[c, :DH, :], ds, 1, 0)

    sweep(backward)
    for s in range(2):
        grad = (acc_dq[s] * (total[s, 0:1, :] * SCALE)).T.astype(BF16)
        for h in range(RATIO):
            dq_ref[s * RUN : (s + 1) * RUN, h * DH : (h + 1) * DH] = grad[h * RUN : (h + 1) * RUN]

    def unsort_chunk(c, carry):
        for j in range(RUNS_CHUNK):
            start = pl.multiple_of(loc[c * RUNS_CHUNK + j] * RUN, RUN)
            dkv_ref[pl.ds(start, RUN), :] = dkvs[c, j * RUN : (j + 1) * RUN, :].astype(BF16)
        return carry

    lax.fori_loop(0, CHUNKS, unsort_chunk, 0)


def attention(own, pb, q, do, kv):
    rows, width = q.shape
    vmem = pl.BlockSpec(memory_space=pltpu.VMEM)
    smem = pl.BlockSpec(memory_space=pltpu.SMEM)
    return pl.pallas_call(
        attention_kernel,
        out_shape=(
            jax.ShapeDtypeStruct((rows, width), BF16),
            jax.ShapeDtypeStruct((rows, width), BF16),
            jax.ShapeDtypeStruct(kv.shape, BF16),
        ),
        in_specs=[smem, smem, vmem, vmem, vmem],
        out_specs=(vmem, vmem, vmem),
        scratch_shapes=[
            pltpu.SMEM((2 * BLOCKS,), jnp.int32),
            pltpu.VMEM((2, ROWS, DH), BF16),
            pltpu.VMEM((2, ROWS, DH), BF16),
            pltpu.VMEM((CHUNKS, CHUNK, 2 * DH), BF16),
            pltpu.VMEM((CHUNKS, 2 * DH, CHUNK), BF16),
            pltpu.VMEM((ITEMS, CHUNK, ROWS), F32),
            pltpu.VMEM((ITEMS, CHUNK, ROWS), BF16),
            pltpu.VMEM((CHUNKS, CHUNK, 2 * DH), F32),
            pltpu.VMEM((2, 8, ROWS), F32),
            pltpu.VMEM((2, 8, ROWS), F32),
            pltpu.VMEM((2, DH, ROWS), F32),
            pltpu.VMEM((2, DH, ROWS), F32),
            pltpu.VMEM((2, ROWS, DH), BF16),
            pltpu.VMEM((2, ROWS, DH), BF16),
            pltpu.VMEM((2, 8, ROWS), F32),
        ],
        compiler_params=pltpu.CompilerParams(vmem_limit_bytes=56 * 1024 * 1024),
    )(own, pb, q, do, kv)


MESH = pl.DeviceIdType.MESH


class Plane:
    def __init__(self, x_count):
        inner, outer = lax.axis_index("inner"), lax.axis_index("outer")
        self.xs = x_count
        self.z_pairs = lax.axis_size("outer") // x_count
        self.zs = 2 * self.z_pairs
        self.x = lax.rem(outer, x_count)
        self.core = lax.rem(inner, 2)
        self.z = 2 * lax.div(outer, x_count) + lax.div(inner, 2)

    def z_off(self, by):
        return lax.rem(self.z + by + self.zs, self.zs)

    def x_off(self, by):
        return lax.rem(self.x + by + self.xs, self.xs)

    def group(self, z, core):
        return (2 * lax.rem(z, 2) + core) * self.z_pairs + lax.div(z, 2)

    def device(self, z=None, core=None, x=None):
        z = self.z if z is None else z
        core = self.core if core is None else core
        x = self.x if x is None else x
        return {"inner": 2 * lax.rem(z, 2) + core, "outer": lax.div(z, 2) * self.xs + x}

    def partners(self):
        found = [self.device(core=1 - self.core)]
        found += [self.device(z=self.z_off(1)), self.device(z=self.z_off(-1))]
        found += [self.device(x=self.x_off(d)) for d in range(1, self.xs)]
        return found

    def greet(self):
        barrier = pltpu.get_barrier_semaphore()
        partners = self.partners()
        for device in partners:
            pl.semaphore_signal(barrier, inc=1, device_id=device, device_id_type=MESH)
        pl.semaphore_wait(barrier, len(partners))


def push(src, dst, send_sem, recv_sem, device):
    copy = pltpu.make_async_remote_copy(
        src_ref=src,
        dst_ref=dst,
        send_sem=send_sem,
        recv_sem=recv_sem,
        device_id=device,
        device_id_type=MESH,
    )
    copy.start()
    return copy


def gather_kernel(
    x_count, own_ref, out_ref, own_sem, x_send, x_recv, z_send, z_recv, c_send, c_recv
):
    at = Plane(x_count)
    far = at.zs // 2
    rows = own_ref.shape[0]
    group_rows = out_ref.shape[1]
    half_rows = group_rows // 2
    at.greet()

    group = at.group(at.z, at.core)
    slot = out_ref.at[group, pl.ds(pl.multiple_of(at.x * rows, rows), rows), :]
    own = pltpu.make_async_copy(own_ref, slot, own_sem)
    own.start()
    sent = [
        push(own_ref, slot, x_send.at[d - 1], x_recv.at[d - 1], at.device(x=at.x_off(d)))
        for d in range(1, at.xs)
    ]
    own.wait()
    for copy in sent:
        copy.wait_recv()

    crossed = []

    def cross(group):
        i = len(crossed)
        whole = out_ref.at[group]
        crossed.append(
            push(whole, whole, c_send.at[i], c_recv.at[i], at.device(core=1 - at.core))
        )

    def along(way, step, group):
        if step == far - 1:
            part = out_ref.at[group, pl.ds(way * half_rows, half_rows), :]
        else:
            part = out_ref.at[group]
        target = at.device(z=at.z_off(1 - 2 * way))
        return push(part, part, z_send.at[way, step], z_recv.at[way, step], target)

    moving = [along(way, 0, group) for way in range(2)]
    cross(group)
    for step in range(far):
        for way in range(2):
            moving[way].wait_recv()
            sent.append(moving[way])
            group = at.group(at.z_off((2 * way - 1) * (step + 1)), at.core)
            if step < far - 1:
                moving[way] = along(way, step + 1, group)
                cross(group)
    cross(group)
    for copy in crossed:
        copy.wait_recv()
    for copy in sent + crossed:
        copy.wait_send()


def gather(x_count, kv):
    rows, width = kv.shape
    z_pairs = lax.axis_size("outer") // x_count
    zs = 2 * z_pairs
    dma = pltpu.SemaphoreType.DMA
    return pl.pallas_call(
        functools.partial(gather_kernel, x_count),
        out_shape=jax.ShapeDtypeStruct((2 * zs, x_count * rows, width), kv.dtype),
        in_specs=[pl.BlockSpec(memory_space=pltpu.VMEM)],
        out_specs=pl.BlockSpec(memory_space=pl.ANY),
        scratch_shapes=[
            dma,
            dma((x_count - 1,)),
            dma((x_count - 1,)),
            dma((2, zs // 2)),
            dma((2, zs // 2)),
            dma((zs,)),
            dma((zs,)),
        ],
        compiler_params=pltpu.CompilerParams(collective_id=0, has_side_effects=True),
    )(kv)


def scatter_kernel(
    x_count,
    part_ref,
    gk_ref,
    gv_ref,
    other,
    held,
    sums,
    total,
    x_out,
    x_in,
    x_send,
    x_recv,
    z_send,
    z_recv,
    c_send,
    c_recv,
):
    at = Plane(x_count)
    far = at.zs // 2
    group_rows = part_ref.shape[1]
    half_rows = group_rows // 2
    rows = gk_ref.shape[0]
    at.greet()

    offsets = [far]
    for step in range(1, far):
        offsets += [far - step, step - far]
    offsets.append(0)
    crossed = [
        push(
            part_ref.at[at.group(at.z_off(offset), 1 - at.core)],
            other.at[i],
            c_send.at[i],
            c_recv.at[i],
            at.device(core=1 - at.core),
        )
        for i, offset in enumerate(offsets)
    ]

    def pair(i):
        crossed[i].wait_recv()
        mine = part_ref[at.group(at.z_off(offsets[i]), at.core)]
        return mine.astype(F32) + other[i].astype(F32)

    def along(way, step):
        place = pl.ds(way * half_rows, half_rows) if step == 0 else pl.ds(0, group_rows)
        return push(
            sums.at[way, step, place, :],
            held.at[way, step, place, :],
            z_send.at[way, step],
            z_recv.at[way, step],
            at.device(z=at.z_off(1 - 2 * way)),
        )

    sent = []
    start = pair(0).astype(BF16)
    moving = []
    for way in range(2):
        place = slice(way * half_rows, (way + 1) * half_rows)
        sums[way, 0, place, :] = start[place]
        moving.append(along(way, 0))
    for step in range(1, far):
        for way in range(2):
            mine = pair(2 * step - 1 + way)
            moving[way].wait_recv()
            sent.append(moving[way])
            if step == 1:
                place = slice(way * half_rows, (way + 1) * half_rows)
                rest = slice((1 - way) * half_rows, (2 - way) * half_rows)
                arrived = held[way, 0, place, :].astype(F32)
                sums[way, 1, place, :] = (mine[place] + arrived).astype(BF16)
                sums[way, 1, rest, :] = mine[rest].astype(BF16)
            else:
                sums[way, step] = (mine + held[way, step - 1].astype(F32)).astype(BF16)
            moving[way] = along(way, step)
    mine = pair(at.zs - 1)
    for way in range(2):
        moving[way].wait_recv()
        sent.append(moving[way])
        mine = mine + held[way, far - 1].astype(F32)
    total[...] = mine
    x_out[...] = mine.astype(BF16)
    across = []
    for d in range(1, at.xs):
        x = at.x_off(d)
        across.append(
            push(
                x_out.at[pl.ds(pl.multiple_of(x * rows, rows), rows), :],
                x_in.at[d - 1],
                x_send.at[d - 1],
                x_recv.at[d - 1],
                at.device(x=x),
            )
        )
    result = total[pl.ds(pl.multiple_of(at.x * rows, rows), rows), :]
    for d in range(1, at.xs):
        across[d - 1].wait_recv()
        result = result + x_in[d - 1].astype(F32)
    gk_ref[...] = result[:, :DH].astype(BF16)
    gv_ref[...] = result[:, DH:].astype(BF16)
    for copy in sent + crossed + across:
        copy.wait_send()


def scatter(x_count, parts):
    groups, group_rows, width = parts.shape
    rows = group_rows // x_count
    far = groups // 4
    vmem = pl.BlockSpec(memory_space=pltpu.VMEM)
    dma = pltpu.SemaphoreType.DMA
    return pl.pallas_call(
        functools.partial(scatter_kernel, x_count),
        out_shape=(jax.ShapeDtypeStruct((rows, DH), BF16),) * 2,
        in_specs=[vmem],
        out_specs=(vmem, vmem),
        scratch_shapes=[
            pltpu.VMEM((2 * far, group_rows, width), BF16),
            pltpu.VMEM((2, far, group_rows, width), BF16),
            pltpu.VMEM((2, far, group_rows, width), BF16),
            pltpu.VMEM((group_rows, width), F32),
            pltpu.VMEM((group_rows, width), BF16),
            pltpu.VMEM((x_count - 1, rows, width), BF16),
            dma((x_count - 1,)),
            dma((x_count - 1,)),
            dma((2, far)),
            dma((2, far)),
            dma((2 * far,)),
            dma((2 * far,)),
        ],
        compiler_params=pltpu.CompilerParams(
            collective_id=1, has_side_effects=True, vmem_limit_bytes=32 * 1024 * 1024
        ),
    )(parts)


def shards(q_rows, k_rows, v_rows, dout, positions):
    heads = lax.axis_size("head")
    tokens = q_rows.shape[0]
    q_width = q_rows.shape[1] // heads
    kv_width = k_rows.shape[1] // heads
    mixed = jnp.concatenate(
        [
            q_rows.reshape(tokens, heads, q_width),
            k_rows.reshape(tokens, heads, kv_width),
            v_rows.reshape(tokens, heads, kv_width),
        ],
        axis=2,
    )
    mine = lax.all_to_all(mixed, "head", split_axis=1, concat_axis=0, tiled=True)
    mine = mine.reshape(heads * tokens, q_width + 2 * kv_width)
    kv = gather(CHIPS_X, mine[:, q_width:])
    own = lax.axis_index("inner") * lax.axis_size("outer") + lax.axis_index("outer")
    pb = positions[:: 2 * RUN] // RUN
    kv_flat = kv.reshape(-1, 2 * kv_width)
    attn_out, grad_q, dkv = attention(own.reshape(1), pb, mine[:, :q_width], dout, kv_flat)
    grad_k, grad_v = scatter(CHIPS_X, dkv.reshape(kv.shape))
    return attn_out, grad_q, grad_k, grad_v


def solution(mesh):
    return jax.shard_map(
        shards,
        mesh=mesh,
        in_specs=(
            P(("inner", "outer", "head"), None),
            P(("inner", "outer", "head"), None),
            P(("inner", "outer", "head"), None),
            P(("inner", "outer"), "head"),
            P(),
        ),
        out_specs=(
            P(("inner", "outer"), "head"),
            P(("inner", "outer"), "head"),
            P(("inner", "outer"), "head"),
            P(("inner", "outer"), "head"),
        ),
        check_vma=False,
    )
```

```python
import functools

import jax
import jax.numpy as jnp
from jax import lax
from jax.experimental import pallas as pl
from jax.experimental.pallas import tpu as pltpu
from jax.sharding import PartitionSpec as P

QH = 32
KVH = 8
DH = 128
RUN = 64
BLOCKS = 64
CHIPS_X = 4
RATIO = QH // KVH
ROWS = RATIO * RUN
CHUNK = 256
RUNS_CHUNK = CHUNK // RUN
CHUNKS = 2 * BLOCKS // RUNS_CHUNK
ITEMS = CHUNKS + 1
LOG2E = 1.4426950408889634
SCALE = DH**-0.5
NEG_FILL = -1e30
F32 = jnp.float32
BF16 = jnp.bfloat16


def dot(a, b, ca, cb):
    return lax.dot_general(a, b, (((ca,), (cb,)), ((), ())), preferred_element_type=F32)


def attention_kernel(
    own_ref,
    pb_ref,
    q_ref,
    do_ref,
    kv_ref,
    out_ref,
    dq_ref,
    dkv_ref,
    loc,
    qs,
    dos,
    kvs,
    kvt,
    scores,
    probs,
    dkvs,
    top,
    total,
    acc_out,
    acc_dq,
    qd,
    dod,
    delta,
):
    own = pb_ref[own_ref[0]]
    first_chunks = own // RUNS_CHUNK

    def place(b, carry):
        p = pb_ref[b]
        loc[p] = b
        loc[2 * BLOCKS - 1 - p] = BLOCKS + b
        return carry

    lax.fori_loop(0, BLOCKS, place, 0)

    for s in range(2):
        rows = slice(s * RUN, (s + 1) * RUN)
        for h in range(RATIO):
            cols = slice(h * DH, (h + 1) * DH)
            qs[s, h * RUN : (h + 1) * RUN, :] = q_ref[rows, cols]
            dos[s, h * RUN : (h + 1) * RUN, :] = do_ref[rows, cols]

    def sort_chunk(c, carry):
        for j in range(RUNS_CHUNK):
            start = pl.multiple_of(loc[c * RUNS_CHUNK + j] * RUN, RUN)
            kvs[c, j * RUN : (j + 1) * RUN, :] = kv_ref[pl.ds(start, RUN), :]
        kvt[c] = kvs[c].T
        dkvs[c] = jnp.zeros((CHUNK, 2 * DH), F32)
        return carry

    lax.fori_loop(0, CHUNKS, sort_chunk, 0)

    top[...] = jnp.full(top.shape, NEG_FILL, F32)
    total[...] = jnp.zeros(total.shape, F32)
    acc_out[...] = jnp.zeros(acc_out.shape, F32)
    acc_dq[...] = jnp.zeros(acc_dq.shape, F32)

    def item(t):
        late = t >= first_chunks
        sel = jnp.where(late, 1, 0)
        return sel, jnp.where(late, t - first_chunks, t)

    def sweep(visit):
        def some(i, carry):
            for j in range(3):
                t = 3 * i + j
                sel, c = item(t)
                visit(t, sel, c, None)
            return carry

        lax.fori_loop(0, (ITEMS - 3) // 3, some, 0)
        sel, c = item(ITEMS - 3)
        visit(ITEMS - 3, sel, c, None)
        visit(ITEMS - 2, 0, first_chunks, own * RUN)
        visit(ITEMS - 1, 1, CHUNKS - 1 - first_chunks, (2 * BLOCKS - 1 - own) * RUN)

    def fold(x, op):
        return op(x.reshape(CHUNK // 8, 8, ROWS), axis=0)

    def score(t, sel, c, first_pos):
        s = dot(kvs[c, :, :DH], qs[sel], 1, 1)
        if first_pos is not None:
            key = c * CHUNK + lax.broadcasted_iota(jnp.int32, (CHUNK, ROWS), 0)
            row = first_pos + lax.rem(lax.broadcasted_iota(jnp.int32, (CHUNK, ROWS), 1), RUN)
            s = jnp.where(key <= row, s, NEG_FILL)
        scores[t] = s
        top[sel] = jnp.maximum(top[sel], fold(s, jnp.max))

    sweep(score)
    for s in range(2):
        m = jnp.max(top[s], axis=0, keepdims=True) * (SCALE * LOG2E)
        top[s] = jnp.broadcast_to(m, (8, ROWS))

    def weigh(t, sel, c, first_pos):
        e = jnp.exp2(scores[t] * (SCALE * LOG2E) - top[sel, 0:1, :])
        total[sel] += fold(e, jnp.sum)
        e = e.astype(BF16)
        probs[t] = e
        acc_out[sel] += dot(kvt[c, DH:, :], e, 1, 0)

    sweep(weigh)
    for s in range(2):
        inv = 1.0 / jnp.sum(total[s], axis=0, keepdims=True)
        out = (acc_out[s] * inv).astype(BF16).astype(F32)
        d_rows = dos[s].astype(F32)
        delta[s] = jnp.broadcast_to(jnp.sum(out * d_rows.T, axis=0, keepdims=True), (8, ROWS))
        total[s] = jnp.broadcast_to(inv, (8, ROWS))
        inv_rows = jnp.broadcast_to(inv, (DH, ROWS)).T
        dod[s] = (d_rows * inv_rows).astype(BF16)
        qd[s] = (qs[s].astype(F32) * (inv_rows * SCALE)).astype(BF16)
        out = out.T.astype(BF16)
        for h in range(RATIO):
            out_ref[s * RUN : (s + 1) * RUN, h * DH : (h + 1) * DH] = out[h * RUN : (h + 1) * RUN]

    def backward(t, sel, c, first_pos):
        e = probs[t]
        dp = dot(kvs[c, :, DH:], dos[sel], 1, 1)
        ds = (e.astype(F32) * (dp - delta[sel, 0:1, :])).astype(BF16)
        dkvs[c, :, DH:] += dot(e, dod[sel], 1, 0)
        dkvs[c, :, :DH] += dot(ds, qd[sel], 1, 0)
        acc_dq[sel] += dot(kvt[c, :DH, :], ds, 1, 0)

    sweep(backward)
    for s in range(2):
        grad = (acc_dq[s] * (total[s, 0:1, :] * SCALE)).T.astype(BF16)
        for h in range(RATIO):
            dq_ref[s * RUN : (s + 1) * RUN, h * DH : (h + 1) * DH] = grad[h * RUN : (h + 1) * RUN]

    def unsort_chunk(c, carry):
        for j in range(RUNS_CHUNK):
            start = pl.multiple_of(loc[c * RUNS_CHUNK + j] * RUN, RUN)
            dkv_ref[pl.ds(start, RUN), :] = dkvs[c, j * RUN : (j + 1) * RUN, :].astype(BF16)
        return carry

    lax.fori_loop(0, CHUNKS, unsort_chunk, 0)


def attention(own, pb, q, do, kv):
    rows, width = q.shape
    vmem = pl.BlockSpec(memory_space=pltpu.VMEM)
    smem = pl.BlockSpec(memory_space=pltpu.SMEM)
    return pl.pallas_call(
        attention_kernel,
        out_shape=(
            jax.ShapeDtypeStruct((rows, width), BF16),
            jax.ShapeDtypeStruct((rows, width), BF16),
            jax.ShapeDtypeStruct(kv.shape, BF16),
        ),
        in_specs=[smem, smem, vmem, vmem, vmem],
        out_specs=(vmem, vmem, vmem),
        scratch_shapes=[
            pltpu.SMEM((2 * BLOCKS,), jnp.int32),
            pltpu.VMEM((2, ROWS, DH), BF16),
            pltpu.VMEM((2, ROWS, DH), BF16),
            pltpu.VMEM((CHUNKS, CHUNK, 2 * DH), BF16),
            pltpu.VMEM((CHUNKS, 2 * DH, CHUNK), BF16),
            pltpu.VMEM((ITEMS, CHUNK, ROWS), F32),
            pltpu.VMEM((ITEMS, CHUNK, ROWS), BF16),
            pltpu.VMEM((CHUNKS, CHUNK, 2 * DH), F32),
            pltpu.VMEM((2, 8, ROWS), F32),
            pltpu.VMEM((2, 8, ROWS), F32),
            pltpu.VMEM((2, DH, ROWS), F32),
            pltpu.VMEM((2, DH, ROWS), F32),
            pltpu.VMEM((2, ROWS, DH), BF16),
            pltpu.VMEM((2, ROWS, DH), BF16),
            pltpu.VMEM((2, 8, ROWS), F32),
        ],
        compiler_params=pltpu.CompilerParams(vmem_limit_bytes=56 * 1024 * 1024),
    )(own, pb, q, do, kv)


MESH = pl.DeviceIdType.MESH


class Plane:
    def __init__(self, x_count):
        inner, outer = lax.axis_index("inner"), lax.axis_index("outer")
        self.xs = x_count
        self.z_pairs = lax.axis_size("outer") // x_count
        self.zs = 2 * self.z_pairs
        self.x = lax.rem(outer, x_count)
        self.core = lax.rem(inner, 2)
        self.z = 2 * lax.div(outer, x_count) + lax.div(inner, 2)

    def z_off(self, by):
        return lax.rem(self.z + by + self.zs, self.zs)

    def x_off(self, by):
        return lax.rem(self.x + by + self.xs, self.xs)

    def group(self, z, core):
        return (2 * lax.rem(z, 2) + core) * self.z_pairs + lax.div(z, 2)

    def device(self, z=None, core=None, x=None):
        z = self.z if z is None else z
        core = self.core if core is None else core
        x = self.x if x is None else x
        return {"inner": 2 * lax.rem(z, 2) + core, "outer": lax.div(z, 2) * self.xs + x}

    def partners(self):
        found = [self.device(core=1 - self.core)]
        found += [self.device(z=self.z_off(1)), self.device(z=self.z_off(-1))]
        found += [self.device(x=self.x_off(d)) for d in range(1, self.xs)]
        return found

    def greet(self, heads=1):
        head = lax.axis_index("head")
        partners = [{"head": lax.rem(head + d, heads)} for d in range(1, heads)]
        partners += self.partners()
        barrier = pltpu.get_barrier_semaphore()
        for device in partners:
            pl.semaphore_signal(barrier, inc=1, device_id=device, device_id_type=MESH)
        pl.semaphore_wait(barrier, len(partners))


def push(src, dst, send_sem, recv_sem, device):
    copy = pltpu.make_async_remote_copy(
        src_ref=src,
        dst_ref=dst,
        send_sem=send_sem,
        recv_sem=recv_sem,
        device_id=device,
        device_id_type=MESH,
    )
    copy.start()
    return copy


def gather_kernel(
    x_count,
    q_ref,
    k_ref,
    v_ref,
    q_out,
    out_ref,
    q_got,
    block,
    own_sem,
    y_send,
    y_recv,
    xa_send,
    xa_recv,
    za_send,
    za_recv,
    ca_send,
    ca_recv,
    xb_send,
    xb_recv,
    zb_send,
    zb_recv,
    cb_send,
    cb_recv,
):
    at = Plane(x_count)
    heads = lax.axis_size("head")
    far = at.zs // 2
    tokens = q_ref.shape[0]
    width = q_ref.shape[1] // heads
    rows = block.shape[0] // 2
    at.greet(heads)

    head = lax.axis_index("head")
    here = pl.ds(pl.multiple_of(head * tokens, tokens), tokens)
    q_moves, kv_moves = [], []
    for d in range(1, heads):
        peer = lax.rem(head + d, heads)
        cols = pl.ds(pl.multiple_of(peer * DH, DH), DH)
        for i, (src, dst) in enumerate(
            (
                (k_ref.at[:, cols], block.at[here, pl.ds(0, DH)]),
                (v_ref.at[:, cols], block.at[here, pl.ds(DH, DH)]),
            )
        ):
            kv_moves.append(
                push(src, dst, y_send.at[i, d - 1], y_recv.at[i, d - 1], {"head": peer})
            )
    for d in range(1, heads):
        peer = lax.rem(head + d, heads)
        cols = pl.ds(pl.multiple_of(peer * width, width), width)
        q_moves.append(
            push(
                q_ref.at[:, cols],
                q_got.at[here, :],
                y_send.at[2, d - 1],
                y_recv.at[2, d - 1],
                {"head": peer},
            )
        )
    cols = pl.ds(pl.multiple_of(head * DH, DH), DH)
    block[here, :DH] = k_ref[:, cols]
    block[here, DH:] = v_ref[:, cols]
    q_got[here, :] = q_ref[:, pl.ds(pl.multiple_of(head * width, width), width)]
    for copy in kv_moves:
        copy.wait_recv()
    sent = kv_moves + q_moves

    mine = pl.ds(pl.multiple_of(at.x * rows, rows), rows)
    group = at.group(at.z, at.core)
    runs = [block.at[pl.ds(half * rows, rows), :] for half in range(2)]
    own = []
    for half in range(2):
        copy = pltpu.make_async_copy(runs[half], out_ref.at[half, group, mine, :], own_sem.at[half])
        copy.start()
        own.append(copy)

    def across(src, dst, send, recv):
        return [
            push(src, dst, send.at[d - 1], recv.at[d - 1], at.device(x=at.x_off(d)))
            for d in range(1, at.xs)
        ]

    def towards(way):
        return at.device(z=at.z_off(1 - 2 * way))

    def move_a(way, step, group):
        size = x_count * rows
        part = out_ref.at[0, group]
        if step == far - 1:
            part = out_ref.at[0, group, pl.ds(way * (size // 2), size // 2), :]
        return push(part, part, za_send.at[way, step], za_recv.at[way, step], towards(way))

    def move_b(way, step, group, src=None):
        if step == far - 1:
            place = pl.ds(pl.multiple_of(at.x * rows + way * (rows // 2), rows // 2), rows // 2)
        else:
            place = mine
        part = out_ref.at[1, group, place, :]
        src = part if src is None else src
        return push(src, part, zb_send.at[way, step], zb_recv.at[way, step], towards(way))

    crossed = []

    def cross(half, i, group):
        whole = out_ref.at[half, group]
        send, recv = (cb_send, cb_recv) if half else (ca_send, ca_recv)
        crossed.append(
            push(whole, whole, send.at[i], recv.at[i], at.device(core=1 - at.core))
        )

    def spread_b(i, group):
        part = out_ref.at[1, group, mine, :]
        return group, i, across(part, part, xb_send.at[i], xb_recv.at[i])

    def finish_b(spread):
        group, i, copies = spread
        for copy in copies:
            copy.wait_recv()
        sent.extend(copies)
        cross(1, i, group)

    first_a = across(runs[0], out_ref.at[0, group, mine, :], xa_send, xa_recv)
    b_moves = [move_b(way, 0, group, runs[1]) for way in range(2)]
    own[1].wait()
    spreads = [spread_b(0, group)]
    own[0].wait()
    for copy in first_a:
        copy.wait_recv()
    sent += first_a
    a_moves = [move_a(way, 0, group) for way in range(2)]
    cross(0, 0, group)
    for step in range(far):
        groups = [at.group(at.z_off((2 * way - 1) * (step + 1)), at.core) for way in range(2)]
        last = step == far - 1
        fresh = []
        for way in range(2):
            b_moves[way].wait_recv()
            sent.append(b_moves[way])
            if not last:
                b_moves[way] = move_b(way, step + 1, groups[way])
                fresh.append(spread_b(2 * step + 1 + way, groups[way]))
        if last:
            fresh.append(spread_b(2 * far - 1, groups[0]))
        for way in range(2):
            a_moves[way].wait_recv()
            sent.append(a_moves[way])
            if not last:
                a_moves[way] = move_a(way, step + 1, groups[way])
                cross(0, 2 * step + 1 + way, groups[way])
        if last:
            cross(0, 2 * far - 1, groups[0])
        for spread in spreads:
            finish_b(spread)
        spreads = fresh
    for spread in spreads:
        finish_b(spread)
    for copy in q_moves:
        copy.wait_recv()
    q_out[...] = q_got[...]
    for copy in crossed:
        copy.wait_recv()
    for copy in sent + crossed:
        copy.wait_send()


def gather(x_count, q_rows, k_rows, v_rows):
    heads = lax.axis_size("head")
    tokens = q_rows.shape[0]
    rows = heads * tokens
    width = q_rows.shape[1] // heads
    z_pairs = lax.axis_size("outer") // x_count
    zs = 2 * z_pairs
    dma = pltpu.SemaphoreType.DMA
    vmem = pl.BlockSpec(memory_space=pltpu.VMEM)
    sems = [(2,), (3, heads - 1), (3, heads - 1)]
    for x_dims in ((x_count - 1,), (zs, x_count - 1)):
        sems += [x_dims, x_dims, (2, zs // 2), (2, zs // 2), (zs,), (zs,)]
    return pl.pallas_call(
        functools.partial(gather_kernel, x_count),
        out_shape=(
            jax.ShapeDtypeStruct((rows, width), BF16),
            jax.ShapeDtypeStruct((2, 2 * zs, x_count * rows // 2, 2 * DH), BF16),
        ),
        in_specs=[vmem, vmem, vmem],
        out_specs=(vmem, pl.BlockSpec(memory_space=pl.ANY)),
        scratch_shapes=[
            pltpu.VMEM((rows, width), BF16),
            pltpu.VMEM((rows, 2 * DH), BF16),
        ]
        + [dma(dims) for dims in sems],
        compiler_params=pltpu.CompilerParams(collective_id=0, has_side_effects=True),
    )(q_rows, k_rows, v_rows)


def scatter_kernel(
    x_count,
    part_ref,
    gk_ref,
    gv_ref,
    other,
    za_in,
    za_out,
    zb_in,
    zb_out,
    xa_in,
    xa_out,
    xb_in,
    xb_out,
    keep,
    xa_send,
    xa_recv,
    za_send,
    za_recv,
    ca_send,
    ca_recv,
    xb_send,
    xb_recv,
    zb_send,
    zb_recv,
    cb_send,
    cb_recv,
):
    at = Plane(x_count)
    far = at.zs // 2
    size = part_ref.shape[2]
    rows = size // x_count
    at.greet()

    offsets = [far]
    for step in range(1, far):
        offsets += [far - step, step - far]
    offsets.append(0)
    crossed = [[], []]
    for i, offset in enumerate(offsets):
        for half in (1, 0):
            send, recv = (cb_send, cb_recv) if half else (ca_send, ca_recv)
            crossed[half].append(
                push(
                    part_ref.at[half, at.group(at.z_off(offset), 1 - at.core)],
                    other.at[half, i],
                    send.at[i],
                    recv.at[i],
                    at.device(core=1 - at.core),
                )
            )

    def pair(half, i):
        crossed[half][i].wait_recv()
        mine = part_ref[half, at.group(at.z_off(offsets[i]), at.core)]
        return mine.astype(F32) + other[half, i].astype(F32)

    sent = []

    def across(src, dst, send, recv):
        copies = []
        for d in range(1, at.xs):
            x = at.x_off(d)
            place = pl.ds(pl.multiple_of(x * rows, rows), rows)
            copies.append(
                push(src.at[place, :], dst.at[d - 1], send.at[d - 1], recv.at[d - 1], at.device(x=x))
            )
        sent.extend(copies)
        return copies

    mine = pl.ds(pl.multiple_of(at.x * rows, rows), rows)

    def spread_b(i):
        total = pair(1, i)
        keep[1, i] = total
        xb_out[i] = total.astype(BF16)
        return across(xb_out.at[i], xb_in.at[i], xb_send.at[i], xb_recv.at[i])

    def collect(copies, kept, arrived):
        total = kept[mine, :]
        for d in range(1, at.xs):
            copies[d - 1].wait_recv()
            total = total + arrived[d - 1].astype(F32)
        return total

    def halves(way, length):
        return pl.ds(way * (length // 2), length // 2)

    def along(out, arrive, send, recv, way, step):
        length = out.shape[2]
        place = halves(way, length) if step == 0 else pl.ds(0, length)
        copy = push(
            out.at[way, step, place, :],
            arrive.at[way, step, place, :],
            send.at[way, step],
            recv.at[way, step],
            at.device(z=at.z_off(1 - 2 * way)),
        )
        sent.append(copy)
        return copy

    def begin(total, out, arrive, send, recv):
        moves = []
        length = out.shape[2]
        for way in range(2):
            out[way, 0, halves(way, length), :] = total[
                way * (length // 2) : (way + 1) * (length // 2)
            ].astype(BF16)
            moves.append(along(out, arrive, send, recv, way, 0))
        return moves

    def go_on(moves, way, step, total, out, arrive, send, recv):
        length = out.shape[2]
        moves[way].wait_recv()
        if step == 1:
            near, rest = way, 1 - way
            part = total[near * (length // 2) : (near + 1) * (length // 2)]
            part = part + arrive[way, 0, halves(near, length), :].astype(F32)
            out[way, 1, halves(near, length), :] = part.astype(BF16)
            out[way, 1, halves(rest, length), :] = total[
                rest * (length // 2) : (rest + 1) * (length // 2)
            ].astype(BF16)
        else:
            out[way, step] = (total + arrive[way, step - 1].astype(F32)).astype(BF16)
        moves[way] = along(out, arrive, send, recv, way, step)

    def end(moves, total, arrive):
        for way in range(2):
            moves[way].wait_recv()
            total = total + arrive[way, far - 1].astype(F32)
        return total

    a_refs = (za_out, za_in, za_send, za_recv)
    b_refs = (zb_out, zb_in, zb_send, zb_recv)
    spreads = {0: spread_b(0)}
    a_moves = begin(pair(0, 0), *a_refs)

    def collect_b(i):
        return collect(spreads[i], keep.at[1, i], xb_in.at[i])

    b_moves = None
    for step in range(1, far):
        for way in range(2):
            spreads[2 * step - 1 + way] = spread_b(2 * step - 1 + way)
        if step == 1:
            b_moves = begin(collect_b(0), *b_refs)
        else:
            for way in range(2):
                go_on(b_moves, way, step - 1, collect_b(2 * step - 3 + way), *b_refs)
        for way in range(2):
            go_on(a_moves, way, step, pair(0, 2 * step - 1 + way), *a_refs)
    spreads[at.zs - 1] = spread_b(at.zs - 1)
    for way in range(2):
        go_on(b_moves, way, far - 1, collect_b(2 * far - 3 + way), *b_refs)
    total = end(a_moves, pair(0, at.zs - 1), za_in)
    keep[0, 0] = total
    xa_out[...] = total.astype(BF16)
    last_a = across(xa_out, xa_in, xa_send, xa_recv)
    second = end(b_moves, collect_b(at.zs - 1), zb_in)
    gk_ref[rows:, :] = second[:, :DH].astype(BF16)
    gv_ref[rows:, :] = second[:, DH:].astype(BF16)
    first = collect(last_a, keep.at[0, 0], xa_in)
    gk_ref[:rows, :] = first[:, :DH].astype(BF16)
    gv_ref[:rows, :] = first[:, DH:].astype(BF16)
    for copy in sent + crossed[0] + crossed[1]:
        copy.wait_send()


def scatter(x_count, parts):
    _, groups, size, width = parts.shape
    rows = size // x_count
    zs = groups // 2
    far = zs // 2
    vmem = pl.BlockSpec(memory_space=pltpu.VMEM)
    dma = pltpu.SemaphoreType.DMA
    sems = []
    for x_dims in ((x_count - 1,), (zs, x_count - 1)):
        sems += [x_dims, x_dims, (2, far), (2, far), (zs,), (zs,)]
    return pl.pallas_call(
        functools.partial(scatter_kernel, x_count),
        out_shape=(jax.ShapeDtypeStruct((2 * rows, DH), BF16),) * 2,
        in_specs=[vmem],
        out_specs=(vmem, vmem),
        scratch_shapes=[
            pltpu.VMEM((2, zs, size, width), BF16),
            pltpu.VMEM((2, far, size, width), BF16),
            pltpu.VMEM((2, far, size, width), BF16),
            pltpu.VMEM((2, far, rows, width), BF16),
            pltpu.VMEM((2, far, rows, width), BF16),
            pltpu.VMEM((x_count - 1, rows, width), BF16),
            pltpu.VMEM((size, width), BF16),
            pltpu.VMEM((zs, x_count - 1, rows, width), BF16),
            pltpu.VMEM((zs, size, width), BF16),
            pltpu.VMEM((2, zs, size, width), F32),
        ]
        + [dma(dims) for dims in sems],
        compiler_params=pltpu.CompilerParams(
            collective_id=1, has_side_effects=True, vmem_limit_bytes=32 * 1024 * 1024
        ),
    )(parts)


def shards(q_rows, k_rows, v_rows, dout, positions):
    queries, kv = gather(CHIPS_X, q_rows, k_rows, v_rows)
    own = lax.axis_index("inner") * lax.axis_size("outer") + lax.axis_index("outer")
    pb = positions[:: 2 * RUN] // RUN
    attn_out, grad_q, dkv = attention(own.reshape(1), pb, queries, dout, kv.reshape(-1, 2 * DH))
    grad_k, grad_v = scatter(CHIPS_X, dkv.reshape(kv.shape))
    return attn_out, grad_q, grad_k, grad_v


def solution(mesh):
    return jax.shard_map(
        shards,
        mesh=mesh,
        in_specs=(
            P(("inner", "outer", "head"), None),
            P(("inner", "outer", "head"), None),
            P(("inner", "outer", "head"), None),
            P(("inner", "outer"), "head"),
            P(),
        ),
        out_specs=(
            P(("inner", "outer"), "head"),
            P(("inner", "outer"), "head"),
            P(("inner", "outer"), "head"),
            P(("inner", "outer"), "head"),
        ),
        check_vma=False,
    )
```

```python
import functools

import jax
import jax.numpy as jnp
from jax import lax
from jax.experimental import pallas as pl
from jax.experimental.pallas import tpu as pltpu
from jax.sharding import PartitionSpec as P

QH = 32
KVH = 8
DH = 128
RUN = 64
BLOCKS = 64
CHIPS_X = 4
RATIO = QH // KVH
ROWS = RATIO * RUN
CHUNK = 256
RUNS_CHUNK = CHUNK // RUN
CHUNKS = 2 * BLOCKS // RUNS_CHUNK
ITEMS = CHUNKS + 1
LOG2E = 1.4426950408889634
SCALE = DH**-0.5
NEG_FILL = -1e30
F32 = jnp.float32
BF16 = jnp.bfloat16


def dot(a, b, ca, cb):
    return lax.dot_general(a, b, (((ca,), (cb,)), ((), ())), preferred_element_type=F32)


MESH = pl.DeviceIdType.MESH


class Plane:
    def __init__(self, x_count):
        inner, outer = lax.axis_index("inner"), lax.axis_index("outer")
        self.xs = x_count
        self.z_pairs = lax.axis_size("outer") // x_count
        self.zs = 2 * self.z_pairs
        self.x = lax.rem(outer, x_count)
        self.core = lax.rem(inner, 2)
        self.z = 2 * lax.div(outer, x_count) + lax.div(inner, 2)

    def z_off(self, by):
        return lax.rem(self.z + by + self.zs, self.zs)

    def x_off(self, by):
        return lax.rem(self.x + by + self.xs, self.xs)

    def group(self, z, core):
        return (2 * lax.rem(z, 2) + core) * self.z_pairs + lax.div(z, 2)

    def device(self, z=None, core=None, x=None):
        z = self.z if z is None else z
        core = self.core if core is None else core
        x = self.x if x is None else x
        return {"inner": 2 * lax.rem(z, 2) + core, "outer": lax.div(z, 2) * self.xs + x}

    def partners(self):
        found = [self.device(core=1 - self.core)]
        found += [self.device(z=self.z_off(1)), self.device(z=self.z_off(-1))]
        found += [self.device(x=self.x_off(d)) for d in range(1, self.xs)]
        return found

    def greet(self, heads=1):
        head = lax.axis_index("head")
        partners = [{"head": lax.rem(head + d, heads)} for d in range(1, heads)]
        partners += self.partners()
        barrier = pltpu.get_barrier_semaphore()
        for device in partners:
            pl.semaphore_signal(barrier, inc=1, device_id=device, device_id_type=MESH)
        pl.semaphore_wait(barrier, len(partners))


def push(src, dst, send_sem, recv_sem, device):
    copy = pltpu.make_async_remote_copy(
        src_ref=src,
        dst_ref=dst,
        send_sem=send_sem,
        recv_sem=recv_sem,
        device_id=device,
        device_id_type=MESH,
    )
    copy.start()
    return copy


def layer_kernel(
    x_count,
    pb_ref,
    q_ref,
    k_ref,
    v_ref,
    do_ref,
    out_ref,
    dq_ref,
    gk_ref,
    gv_ref,
    q_got,
    block,
    kv,
    qs,
    dos,
    s_full,
    s_mix,
    e_full,
    e_mix,
    e_own,
    top,
    peak,
    total,
    marks,
    acc_out,
    acc_dq,
    qd,
    dod,
    delta,
    parts,
    other,
    za_in,
    za_out,
    zb_in,
    zb_out,
    xa_in,
    xa_out,
    xb_in,
    xb_out,
    keep,
    y_send,
    y_recv,
    *sems,
):
    at = Plane(x_count)
    heads = lax.axis_size("head")
    far = at.zs // 2
    tokens = q_ref.shape[0]
    width = q_ref.shape[1] // heads
    rows = block.shape[0] // 2
    size = x_count * rows
    ga, gb, sa, sb = (sems[6 * i : 6 * i + 6] for i in range(4))
    at.greet(heads)

    head = lax.axis_index("head")
    here = pl.ds(pl.multiple_of(head * tokens, tokens), tokens)
    q_moves, kv_moves = [], []
    for d in range(1, heads):
        peer = lax.rem(head + d, heads)
        cols = pl.ds(pl.multiple_of(peer * DH, DH), DH)
        for i, src in enumerate((k_ref, v_ref)):
            kv_moves.append(
                push(
                    src.at[:, cols],
                    block.at[here, pl.ds(i * DH, DH)],
                    y_send.at[i, d - 1],
                    y_recv.at[i, d - 1],
                    {"head": peer},
                )
            )
    for d in range(1, heads):
        peer = lax.rem(head + d, heads)
        cols = pl.ds(pl.multiple_of(peer * width, width), width)
        q_moves.append(
            push(
                q_ref.at[:, cols],
                q_got.at[here, :],
                y_send.at[2, d - 1],
                y_recv.at[2, d - 1],
                {"head": peer},
            )
        )
    cols = pl.ds(pl.multiple_of(head * DH, DH), DH)
    block[here, :DH] = k_ref[:, cols]
    block[here, DH:] = v_ref[:, cols]
    q_got[here, :] = q_ref[:, pl.ds(pl.multiple_of(head * width, width), width)]
    for copy in kv_moves:
        copy.wait_recv()
    sent = kv_moves + q_moves

    mine = pl.ds(pl.multiple_of(at.x * rows, rows), rows)
    own = at.group(at.z, at.core)
    kv[0, own, mine, :] = block[:rows, :]
    kv[1, own, mine, :] = block[rows:, :]

    def towards(way):
        return at.device(z=at.z_off(1 - 2 * way))

    def beside(src, dst, send, recv):
        copies = [
            push(src, dst, send.at[d - 1], recv.at[d - 1], at.device(x=at.x_off(d)))
            for d in range(1, at.xs)
        ]
        sent.extend(copies)
        return copies

    def arrive(copies):
        for copy in copies:
            copy.wait_recv()

    def move_a(way, step, group):
        part = kv.at[0, group]
        if step == far - 1:
            part = kv.at[0, group, pl.ds(way * (size // 2), size // 2), :]
        copy = push(part, part, ga[2].at[way, step], ga[3].at[way, step], towards(way))
        sent.append(copy)
        return copy

    def move_b(way, step, group):
        place = mine
        if step == far - 1:
            place = pl.ds(pl.multiple_of(at.x * rows + way * (rows // 2), rows // 2), rows // 2)
        part = kv.at[1, group, place, :]
        copy = push(part, part, gb[2].at[way, step], gb[3].at[way, step], towards(way))
        sent.append(copy)
        return copy

    crosses = {}

    def cross(half, i, group):
        whole = kv.at[half, group]
        send, recv = (gb, ga)[1 - half][4:]
        copy = push(whole, whole, send.at[i], recv.at[i], at.device(core=1 - at.core))
        sent.append(copy)
        crosses[half, i] = copy

    def spread(i, group):
        part = kv.at[1, group, mine, :]
        return i, group, beside(part, part, gb[0].at[i], gb[1].at[i])

    def finish(spreads):
        for i, group, copies in spreads:
            arrive(copies)
            cross(1, i, group)

    def fold(x, op):
        return op(x.reshape(x.shape[0] // 8, 8, ROWS), axis=0)

    def gap(group, r):
        return pb_ref[x_count * own + at.x] - pb_ref[x_count * group + r]

    def early(group, r):
        return jnp.full((RUN, ROWS), gap(group, r), jnp.int32) >= 0

    def run(r):
        return slice(r * RUN, (r + 1) * RUN)

    def products(group, half, rows_ref):
        first, second = kv[0, group], kv[1, group]
        cols = slice(half * DH, (half + 1) * DH)
        return (
            dot(first[:, cols], rows_ref[1], 1, 1),
            dot(first[:, cols], rows_ref[0], 1, 1),
            dot(second[:, cols], rows_ref[1], 1, 1),
        )

    def score(slot, group):
        full, one, two = products(group, 0, qs)
        s_full[slot] = full
        tops = [top[0], jnp.maximum(top[1], fold(full, jnp.max))]
        for r in range(x_count):
            is_early = early(group, r)
            mix = jnp.where(is_early, one[run(r)], two[run(r)])
            s_mix[slot, run(r), :] = mix
            highest = fold(mix, jnp.max)
            tops[0] = jnp.maximum(tops[0], jnp.where(is_early[:8], highest, NEG_FILL))
            tops[1] = jnp.maximum(tops[1], jnp.where(is_early[:8], NEG_FILL, highest))
        top[0], top[1] = tops

    def score_own():
        full, one, two = products(own, 0, qs)
        s_full[0] = full
        key = lax.broadcasted_iota(jnp.int32, (RUN, ROWS), 0)
        row = lax.rem(lax.broadcasted_iota(jnp.int32, (RUN, ROWS), 1), RUN)
        tops = [top[0], jnp.maximum(top[1], fold(full, jnp.max))]
        for r in range(x_count):
            away = gap(own, r) * RUN
            for s, (tile, sign) in enumerate(((one, 1), (two, -1))):
                masked = jnp.where(key - row <= sign * away, tile[run(r)], NEG_FILL)
                s_mix[s, run(r), :] = masked
                tops[s] = jnp.maximum(tops[s], fold(masked, jnp.max))
        top[0], top[1] = tops

    def renew(batch):
        for s in range(2):
            highest = jnp.max(top[s], axis=0, keepdims=True)
            factor = jnp.exp2((peak[s, 0:1, :] - highest) * (SCALE * LOG2E))
            total[s] = total[s] * factor
            acc_out[s] = acc_out[s] * factor
            peak[s] = jnp.broadcast_to(highest, (8, ROWS))
            marks[batch, s] = jnp.broadcast_to(highest, (8, ROWS))

    def weigh(slot, group):
        highs = [peak[s, 0:1, :] * (SCALE * LOG2E) for s in range(2)]
        full = jnp.exp2(s_full[slot] * (SCALE * LOG2E) - highs[1])
        totals = [total[0], total[1] + fold(full, jnp.sum)]
        full = full.astype(BF16)
        e_full[group] = full
        ones, twos = [], []
        for r in range(x_count):
            is_early = early(group, r)
            high = jnp.where(is_early[:8], highs[0], highs[1])[0:1]
            e = jnp.exp2(s_mix[slot, run(r), :] * (SCALE * LOG2E) - high)
            e_mix[group, run(r), :] = e.astype(BF16)
            ones.append(jnp.where(is_early, e, 0.0))
            twos.append(jnp.where(is_early, 0.0, e))
            totals[0] = totals[0] + fold(ones[-1], jnp.sum)
            totals[1] = totals[1] + fold(twos[-1], jnp.sum)
        total[0], total[1] = totals
        add_out(group, full, ones, twos)

    def weigh_own():
        full = jnp.exp2((s_full[0] - peak[1, 0:1, :]) * (SCALE * LOG2E))
        one = jnp.exp2((s_mix[0] - peak[0, 0:1, :]) * (SCALE * LOG2E))
        two = jnp.exp2((s_mix[1] - peak[1, 0:1, :]) * (SCALE * LOG2E))
        total[0] = total[0] + fold(one, jnp.sum)
        total[1] = total[1] + fold(full, jnp.sum) + fold(two, jnp.sum)
        full = full.astype(BF16)
        e_full[own] = full
        e_own[0] = one.astype(BF16)
        e_own[1] = two.astype(BF16)
        add_out(own, full, [one], [two])

    def add_out(group, full, ones, twos):
        one = jnp.concatenate([e.astype(BF16) for e in ones], axis=0)
        two = jnp.concatenate([e.astype(BF16) for e in twos], axis=0)
        first = kv[0, group, :, DH:].T
        second = kv[1, group, :, DH:].T
        acc_out[0] = acc_out[0] + dot(first, one, 1, 0)
        acc_out[1] = acc_out[1] + dot(first, full, 1, 0) + dot(second, two, 1, 0)

    def forward(batch, count, group_of):
        def first(j, carry):
            score(j, group_of(j))
            return carry

        def then(j, carry):
            weigh(j, group_of(j))
            return carry

        lax.fori_loop(0, count, first, 0)
        renew(batch)
        lax.fori_loop(0, count, then, 0)

    a_first = beside(kv.at[0, own, mine, :], kv.at[0, own, mine, :], ga[0], ga[1])
    b_moves = [move_b(way, 0, own) for way in range(2)]
    spreads = [spread(0, own)]
    arrive(a_first)
    a_moves = [move_a(way, 0, own) for way in range(2)]
    cross(0, 0, own)
    arrive(q_moves)
    for s in range(2):
        for h in range(RATIO):
            cols = slice(h * DH, (h + 1) * DH)
            qs[s, run(h), :] = q_got[run(s), cols]
            dos[s, run(h), :] = do_ref[run(s), cols]
    top[...] = jnp.full(top.shape, NEG_FILL, F32)
    peak[...] = jnp.full(peak.shape, NEG_FILL, F32)
    total[...] = jnp.zeros(total.shape, F32)
    acc_out[...] = jnp.zeros(acc_out.shape, F32)
    acc_dq[...] = jnp.zeros(acc_dq.shape, F32)
    finish(spreads)
    score_own()
    renew(0)
    weigh_own()

    def both(by):
        return lambda j: at.group(
            at.z_off(by * (2 * lax.rem(j, 2) - 1)), lax.rem(at.core + lax.div(j, 2), 2)
        )

    def crossed(indices):
        for i in indices:
            for half in range(2):
                crosses[half, i].wait_recv()

    for step in range(far):
        groups = [at.group(at.z_off((2 * way - 1) * (step + 1)), at.core) for way in range(2)]
        last = step == far - 1
        spreads = []
        arrive(b_moves)
        if last:
            spreads.append(spread(2 * far - 1, groups[0]))
        else:
            b_moves = [move_b(way, step + 1, groups[way]) for way in range(2)]
            spreads = [spread(2 * step + 1 + way, groups[way]) for way in range(2)]
        if last:
            arrive(a_moves)
            cross(0, 2 * far - 1, groups[0])
        else:
            for way in range(2):
                a_moves[way].wait_recv()
                a_moves[way] = move_a(way, step + 1, groups[way])
                cross(0, 2 * step + 1 + way, groups[way])
        if step == 0:
            crossed([0])
            forward(1, 1, lambda j: at.group(at.z, 1 - at.core))
        else:
            crossed([2 * step - 1, 2 * step])
            forward(1 + step, 4, both(step))
        finish(spreads)
    crossed([2 * far - 1])
    forward(1 + far, 2, lambda j: at.group(at.z_off(far), lax.rem(at.core + j, 2)))

    for s in range(2):
        inv = 1.0 / jnp.sum(total[s], axis=0, keepdims=True)
        out = (acc_out[s] * inv).astype(BF16).astype(F32)
        d_rows = dos[s].astype(F32)
        q_part = qs[s].astype(F32) * SCALE
        delta[s] = jnp.broadcast_to(jnp.sum(out * d_rows.T, axis=0, keepdims=True), (8, ROWS))
        total[s] = jnp.broadcast_to(inv, (8, ROWS))
        for batch in range(far + 2):
            factor = jnp.exp2((marks[batch, s] - peak[s]) * (SCALE * LOG2E))
            marks[batch, s] = factor
            by_row = jnp.broadcast_to(factor[0:1] * inv, (DH, ROWS)).T
            dod[batch, s] = (d_rows * by_row).astype(BF16)
            qd[batch, s] = (q_part * by_row).astype(BF16)
        out = out.T.astype(BF16)
        for h in range(RATIO):
            out_ref[run(s), h * DH : (h + 1) * DH] = out[run(h)]

    def backward(group, batch, who, i, is_own=False):
        pf, p1, p2 = products(group, 1, dos)
        full = e_full[group]
        d_one, d_two = delta[0, 0:1, :], delta[1, 0:1, :]
        ds_full = (full.astype(F32) * (pf - d_two)).astype(BF16)
        if is_own:
            one, two = e_own[0], e_own[1]
            ds_one = (one.astype(F32) * (p1 - d_one)).astype(BF16)
            ds_two = (two.astype(F32) * (p2 - d_two)).astype(BF16)
        else:
            lists = [[], [], [], []]
            for r in range(x_count):
                is_early = early(group, r)
                e = e_mix[group, run(r), :].astype(F32)
                ds = e * jnp.where(is_early, p1[run(r)] - d_one, p2[run(r)] - d_two)
                for x, (to_one, to_two) in ((e, lists[:2]), (ds, lists[2:])):
                    to_one.append(jnp.where(is_early, x, 0.0).astype(BF16))
                    to_two.append(jnp.where(is_early, 0.0, x).astype(BF16))
            one, two, ds_one, ds_two = (jnp.concatenate(x, axis=0) for x in lists)
        parts[who, 0, i, :, :DH] = (
            dot(ds_full, qd[batch, 1], 1, 0) + dot(ds_one, qd[batch, 0], 1, 0)
        ).astype(BF16)
        parts[who, 0, i, :, DH:] = (
            dot(full, dod[batch, 1], 1, 0) + dot(one, dod[batch, 0], 1, 0)
        ).astype(BF16)
        parts[who, 1, i, :, :DH] = dot(ds_two, qd[batch, 1], 1, 0).astype(BF16)
        parts[who, 1, i, :, DH:] = dot(two, dod[batch, 1], 1, 0).astype(BF16)
        first = kv[0, group, :, :DH].T
        second = kv[1, group, :, :DH].T
        acc_dq[0] = acc_dq[0] + marks[batch, 0, 0:1, :] * dot(first, ds_one, 1, 0)
        acc_dq[1] = acc_dq[1] + marks[batch, 1, 0:1, :] * (
            dot(first, ds_full, 1, 0) + dot(second, ds_two, 1, 0)
        )

    hand_over = {}

    def give(i):
        for half in (1, 0):
            send, recv = (sb, sa)[1 - half][4:]
            copy = push(
                parts.at[0, half, i],
                other.at[half, i],
                send.at[i],
                recv.at[i],
                at.device(core=1 - at.core),
            )
            sent.append(copy)
            hand_over[half, i] = copy

    def pair(half, i):
        hand_over[half, i].wait_recv()
        return parts[1, half, i].astype(F32) + other[half, i].astype(F32)

    def across(src, dst, send, recv):
        copies = []
        for d in range(1, at.xs):
            x = at.x_off(d)
            place = pl.ds(pl.multiple_of(x * rows, rows), rows)
            copies.append(
                push(src.at[place, :], dst.at[d - 1], send.at[d - 1], recv.at[d - 1], at.device(x=x))
            )
        sent.extend(copies)
        return copies

    def spread_b(i):
        both_cores = pair(1, i)
        keep[i] = both_cores
        xb_out[i] = both_cores.astype(BF16)
        return across(xb_out.at[i], xb_in.at[i], sb[0].at[i], sb[1].at[i])

    def collect(copies, kept, arrived):
        summed = kept[mine, :]
        for d in range(1, at.xs):
            copies[d - 1].wait_recv()
            summed = summed + arrived[d - 1].astype(F32)
        return summed

    def collect_b(i):
        return collect(b_spreads[i], keep.at[i], xb_in.at[i])

    def half_of(way, length):
        return slice(way * (length // 2), (way + 1) * (length // 2))

    def along(out, into, sems, way, step):
        length = out.shape[2]
        place = pl.ds(way * (length // 2), length // 2) if step == 0 else pl.ds(0, length)
        copy = push(
            out.at[way, step, place, :],
            into.at[way, step, place, :],
            sems[2].at[way, step],
            sems[3].at[way, step],
            towards(way),
        )
        sent.append(copy)
        return copy

    def begin(summed, out, into, sems):
        moves = []
        for way in range(2):
            place = half_of(way, out.shape[2])
            out[way, 0, place, :] = summed[place].astype(BF16)
            moves.append(along(out, into, sems, way, 0))
        return moves

    def go_on(moves, way, step, summed, out, into, sems):
        moves[way].wait_recv()
        if step == 1:
            near, rest = half_of(way, out.shape[2]), half_of(1 - way, out.shape[2])
            out[way, 1, near, :] = (summed[near] + into[way, 0, near, :].astype(F32)).astype(BF16)
            out[way, 1, rest, :] = summed[rest].astype(BF16)
        else:
            out[way, step] = (summed + into[way, step - 1].astype(F32)).astype(BF16)
        moves[way] = along(out, into, sems, way, step)

    def end(moves, summed, into):
        for way in range(2):
            moves[way].wait_recv()
            summed = summed + into[way, far - 1].astype(F32)
        return summed

    def back(who, step):
        core = lax.rem(at.core + 1 + who, 2)

        def one_way(way, carry):
            offset = (far - step) * (1 - 2 * way)
            group = at.group(at.z_off(offset), core)
            backward(group, 1 + far - step, who, 2 * step - 1 + way)
            return carry

        lax.fori_loop(0, 2, one_way, 0)

    a_refs = (za_out, za_in, sa)
    b_refs = (zb_out, zb_in, sb)
    backward(at.group(at.z_off(far), 1 - at.core), 1 + far, 0, 0)
    give(0)
    backward(at.group(at.z_off(far), at.core), 1 + far, 1, 0)
    b_spreads = {0: spread_b(0)}
    a_moves = begin(pair(0, 0), *a_refs)
    b_moves = None
    for step in range(1, far):
        back(0, step)
        give(2 * step - 1)
        give(2 * step)
        back(1, step)
        for way in range(2):
            b_spreads[2 * step - 1 + way] = spread_b(2 * step - 1 + way)
        for way in range(2):
            go_on(a_moves, way, step, pair(0, 2 * step - 1 + way), *a_refs)
        if step == 1:
            b_moves = begin(collect_b(0), *b_refs)
        else:
            for way in range(2):
                go_on(b_moves, way, step - 1, collect_b(2 * step - 3 + way), *b_refs)
    backward(at.group(at.z, 1 - at.core), 1, 0, at.zs - 1)
    give(at.zs - 1)
    for way in range(2):
        go_on(b_moves, way, far - 1, collect_b(2 * far - 3 + way), *b_refs)
    backward(own, 0, 1, at.zs - 1, True)
    b_spreads[at.zs - 1] = spread_b(at.zs - 1)
    mine_a = end(a_moves, pair(0, at.zs - 1), za_in)
    other_a = keep.at[0]
    other_a[...] = mine_a
    xa_out[...] = mine_a.astype(BF16)
    last_a = across(xa_out, xa_in, sa[0], sa[1])
    for s in range(2):
        grad = (acc_dq[s] * (total[s, 0:1, :] * SCALE)).T.astype(BF16)
        for h in range(RATIO):
            dq_ref[run(s), h * DH : (h + 1) * DH] = grad[run(h)]
    second = end(b_moves, collect_b(at.zs - 1), zb_in)
    gk_ref[rows:, :] = second[:, :DH].astype(BF16)
    gv_ref[rows:, :] = second[:, DH:].astype(BF16)
    first = collect(last_a, keep.at[0], xa_in)
    gk_ref[:rows, :] = first[:, :DH].astype(BF16)
    gv_ref[:rows, :] = first[:, DH:].astype(BF16)
    for copy in sent:
        copy.wait_send()


def layer(x_count, pb, q_rows, k_rows, v_rows, dout):
    heads = lax.axis_size("head")
    rows = heads * q_rows.shape[0]
    width = q_rows.shape[1] // heads
    zs = 2 * (lax.axis_size("outer") // x_count)
    far = zs // 2
    run = rows // 2
    size = x_count * run
    batches = far + 2
    kv_width = 2 * DH
    dma = pltpu.SemaphoreType.DMA
    vmem = pl.BlockSpec(memory_space=pltpu.VMEM)
    sems = [(3, heads - 1), (3, heads - 1)]
    for x_dims in ((x_count - 1,), (zs, x_count - 1)) * 2:
        sems += [x_dims, x_dims, (2, far), (2, far), (zs,), (zs,)]
    buffers = [
        ((rows, width), BF16),
        ((rows, kv_width), BF16),
        ((2, 2 * zs, size, kv_width), BF16),
        ((2, ROWS, DH), BF16),
        ((2, ROWS, DH), BF16),
        ((4, size, ROWS), F32),
        ((4, size, ROWS), F32),
        ((2 * zs, size, ROWS), BF16),
        ((2 * zs, size, ROWS), BF16),
        ((2, size, ROWS), BF16),
        ((2, 8, ROWS), F32),
        ((2, 8, ROWS), F32),
        ((2, 8, ROWS), F32),
        ((batches, 2, 8, ROWS), F32),
        ((2, DH, ROWS), F32),
        ((2, DH, ROWS), F32),
        ((batches, 2, ROWS, DH), BF16),
        ((batches, 2, ROWS, DH), BF16),
        ((2, 8, ROWS), F32),
        ((2, 2, zs, size, kv_width), BF16),
        ((2, zs, size, kv_width), BF16),
        ((2, far, size, kv_width), BF16),
        ((2, far, size, kv_width), BF16),
        ((2, far, run, kv_width), BF16),
        ((2, far, run, kv_width), BF16),
        ((x_count - 1, run, kv_width), BF16),
        ((size, kv_width), BF16),
        ((zs, x_count - 1, run, kv_width), BF16),
        ((zs, size, kv_width), BF16),
        ((zs, size, kv_width), F32),
    ]
    return pl.pallas_call(
        functools.partial(layer_kernel, x_count),
        out_shape=(jax.ShapeDtypeStruct((rows, width), BF16),) * 2
        + (jax.ShapeDtypeStruct((rows, DH), BF16),) * 2,
        in_specs=[pl.BlockSpec(memory_space=pltpu.SMEM)] + [vmem] * 4,
        out_specs=(vmem,) * 4,
        scratch_shapes=[pltpu.VMEM(dims, kind) for dims, kind in buffers]
        + [dma(dims) for dims in sems],
        compiler_params=pltpu.CompilerParams(
            collective_id=0, has_side_effects=True, vmem_limit_bytes=56 * 1024 * 1024
        ),
    )(pb, q_rows, k_rows, v_rows, dout)


def shards(q_rows, k_rows, v_rows, dout, positions):
    return layer(CHIPS_X, positions[:: 2 * RUN] // RUN, q_rows, k_rows, v_rows, dout)


def solution(mesh):
    return jax.shard_map(
        shards,
        mesh=mesh,
        in_specs=(
            P(("inner", "outer", "head"), None),
            P(("inner", "outer", "head"), None),
            P(("inner", "outer", "head"), None),
            P(("inner", "outer"), "head"),
            P(),
        ),
        out_specs=(
            P(("inner", "outer"), "head"),
            P(("inner", "outer"), "head"),
            P(("inner", "outer"), "head"),
            P(("inner", "outer"), "head"),
        ),
        check_vma=False,
    )
```

```python
import functools

import jax
import jax.numpy as jnp
from jax import lax
from jax.experimental import pallas as pl
from jax.experimental.pallas import tpu as pltpu
from jax.sharding import PartitionSpec as P

QH = 32
KVH = 8
DH = 128
RUN = 64
BLOCKS = 64
CHIPS_X = 4
RATIO = QH // KVH
ROWS = RATIO * RUN
CHUNK = 256
RUNS_CHUNK = CHUNK // RUN
CHUNKS = 2 * BLOCKS // RUNS_CHUNK
ITEMS = CHUNKS + 1
LOG2E = 1.4426950408889634
SCALE = DH**-0.5
NEG_FILL = -1e30
F32 = jnp.float32
BF16 = jnp.bfloat16


def dot(a, b, ca, cb):
    return lax.dot_general(a, b, (((ca,), (cb,)), ((), ())), preferred_element_type=F32)


MESH = pl.DeviceIdType.MESH


class Plane:
    def __init__(self, x_count):
        inner, outer = lax.axis_index("inner"), lax.axis_index("outer")
        self.xs = x_count
        self.z_pairs = lax.axis_size("outer") // x_count
        self.zs = 2 * self.z_pairs
        self.x = lax.rem(outer, x_count)
        self.core = lax.rem(inner, 2)
        self.z = 2 * lax.div(outer, x_count) + lax.div(inner, 2)

    def z_off(self, by):
        return lax.rem(self.z + by + self.zs, self.zs)

    def x_off(self, by):
        return lax.rem(self.x + by + self.xs, self.xs)

    def group(self, z, core):
        return (2 * lax.rem(z, 2) + core) * self.z_pairs + lax.div(z, 2)

    def device(self, z=None, core=None, x=None):
        z = self.z if z is None else z
        core = self.core if core is None else core
        x = self.x if x is None else x
        return {"inner": 2 * lax.rem(z, 2) + core, "outer": lax.div(z, 2) * self.xs + x}

    def partners(self):
        found = [self.device(core=1 - self.core)]
        found += [self.device(z=self.z_off(1)), self.device(z=self.z_off(-1))]
        found += [self.device(x=self.x_off(d)) for d in range(1, self.xs)]
        return found

    def greet(self, heads=1):
        head = lax.axis_index("head")
        partners = [{"head": lax.rem(head + d, heads)} for d in range(1, heads)]
        partners += self.partners()
        barrier = pltpu.get_barrier_semaphore()
        for device in partners:
            pl.semaphore_signal(barrier, inc=1, device_id=device, device_id_type=MESH)
        pl.semaphore_wait(barrier, len(partners))


def push(src, dst, send_sem, recv_sem, device):
    copy = pltpu.make_async_remote_copy(
        src_ref=src,
        dst_ref=dst,
        send_sem=send_sem,
        recv_sem=recv_sem,
        device_id=device,
        device_id_type=MESH,
    )
    copy.start()
    return copy


def layer_kernel(
    x_count,
    pos_ref,
    q_ref,
    k_ref,
    v_ref,
    do_ref,
    out_ref,
    dq_ref,
    gk_ref,
    gv_ref,
    q_got,
    block,
    kv,
    qs,
    dos,
    s_full,
    s_mix,
    e_full,
    e_mix,
    e_own,
    km,
    vm,
    km_t,
    ka_t,
    dp_full,
    dp_mix,
    vm_t,
    top,
    peak,
    total,
    marks,
    acc_out,
    acc_dq,
    qd,
    dod,
    delta,
    parts,
    other,
    za_in,
    za_out,
    zb_in,
    zb_out,
    xa_in,
    xa_out,
    xb_in,
    xb_out,
    keep,
    y_send,
    y_recv,
    *sems,
):
    at = Plane(x_count)
    heads = lax.axis_size("head")
    far = at.zs // 2
    tokens = q_ref.shape[0]
    width = q_ref.shape[1] // heads
    rows = block.shape[0] // 2
    size = x_count * rows
    ga, gb, sa, sb = (sems[6 * i : 6 * i + 6] for i in range(4))
    at.greet(heads)

    head = lax.axis_index("head")
    here = pl.ds(pl.multiple_of(head * tokens, tokens), tokens)
    q_moves, kv_moves = [], []
    for d in range(1, heads):
        peer = lax.rem(head + d, heads)
        cols = pl.ds(pl.multiple_of(peer * DH, DH), DH)
        for i, src in enumerate((k_ref, v_ref)):
            kv_moves.append(
                push(
                    src.at[:, cols],
                    block.at[here, pl.ds(i * DH, DH)],
                    y_send.at[i, d - 1],
                    y_recv.at[i, d - 1],
                    {"head": peer},
                )
            )
    for d in range(1, heads):
        peer = lax.rem(head + d, heads)
        cols = pl.ds(pl.multiple_of(peer * width, width), width)
        q_moves.append(
            push(
                q_ref.at[:, cols],
                q_got.at[here, :],
                y_send.at[2, d - 1],
                y_recv.at[2, d - 1],
                {"head": peer},
            )
        )
    cols = pl.ds(pl.multiple_of(head * DH, DH), DH)
    block[here, :DH] = k_ref[:, cols]
    block[here, DH:] = v_ref[:, cols]
    q_got[here, :] = q_ref[:, pl.ds(pl.multiple_of(head * width, width), width)]
    for copy in kv_moves:
        copy.wait_recv()
    sent = kv_moves + q_moves

    mine = pl.ds(pl.multiple_of(at.x * rows, rows), rows)
    own = at.group(at.z, at.core)
    kv[0, own, mine, :] = block[:rows, :]
    kv[1, own, mine, :] = block[rows:, :]

    def towards(way):
        return at.device(z=at.z_off(1 - 2 * way))

    def beside(src, dst, send, recv):
        copies = [
            push(src, dst, send.at[d - 1], recv.at[d - 1], at.device(x=at.x_off(d)))
            for d in range(1, at.xs)
        ]
        sent.extend(copies)
        return copies

    def arrive(copies):
        for copy in copies:
            copy.wait_recv()

    def move_a(way, step, group):
        part = kv.at[0, group]
        if step == far - 1:
            part = kv.at[0, group, pl.ds(way * (size // 2), size // 2), :]
        copy = push(part, part, ga[2].at[way, step], ga[3].at[way, step], towards(way))
        sent.append(copy)
        return copy

    def move_b(way, step, group):
        place = mine
        if step == far - 1:
            place = pl.ds(pl.multiple_of(at.x * rows + way * (rows // 2), rows // 2), rows // 2)
        part = kv.at[1, group, place, :]
        copy = push(part, part, gb[2].at[way, step], gb[3].at[way, step], towards(way))
        sent.append(copy)
        return copy

    crosses = {}

    def cross(half, i, group):
        whole = kv.at[half, group]
        send, recv = (gb, ga)[1 - half][4:]
        copy = push(whole, whole, send.at[i], recv.at[i], at.device(core=1 - at.core))
        sent.append(copy)
        crosses[half, i] = copy

    def spread(i, group):
        part = kv.at[1, group, mine, :]
        return i, group, beside(part, part, gb[0].at[i], gb[1].at[i])

    def finish(spreads):
        for i, group, copies in spreads:
            arrive(copies)
            cross(1, i, group)

    def fold(x, op):
        return op(x.reshape(x.shape[0] // 8, 8, ROWS), axis=0)

    def gap(group, r):
        mine_first = pos_ref[(x_count * own + at.x) * 2 * rows]
        return mine_first - pos_ref[(x_count * group + r) * 2 * rows]

    def early(group, r, shape=(RUN, ROWS)):
        return jnp.full(shape, gap(group, r), jnp.int32) >= 0

    def run(r):
        return slice(r * RUN, (r + 1) * RUN)

    def prepare(group):
        first, second = kv[0, group], kv[1, group]
        for r in range(x_count):
            is_early = early(group, r, (RUN, 2 * DH))
            left = jnp.where(is_early, first[run(r)].astype(F32), 0.0).astype(BF16)
            right = jnp.where(is_early, 0.0, second[run(r)].astype(F32)).astype(BF16)
            km[group, run(r), :] = jnp.concatenate([left[:, :DH], right[:, :DH]], axis=1)
            vm[run(r), :] = jnp.concatenate([left[:, DH:], right[:, DH:]], axis=1)
        km_t[group] = km[group].T
        ka_t[group] = first[:, :DH].T
        dp_full[group] = dot(first[:, DH:], dos[:, DH:], 1, 1)
        dp_mix[group] = dot(vm[...], dos[...], 1, 1)
        return vm[...].T

    def score(slot, group):
        full = dot(kv[0, group, :, :DH], qs[:, DH:], 1, 1)
        vm_t[slot] = prepare(group)
        mix = dot(km[group], qs[...], 1, 1)
        s_full[slot] = full
        s_mix[slot] = mix
        tops = [top[0], jnp.maximum(top[1], fold(full, jnp.max))]
        for r in range(x_count):
            is_early = early(group, r, (8, ROWS))
            highest = fold(mix[run(r)], jnp.max)
            tops[0] = jnp.maximum(tops[0], jnp.where(is_early, highest, NEG_FILL))
            tops[1] = jnp.maximum(tops[1], jnp.where(is_early, NEG_FILL, highest))
        top[0], top[1] = tops

    def score_own():
        first, second = kv[0, own, :, :DH], kv[1, own, :, :DH]
        full = dot(first, qs[:, DH:], 1, 1)
        one = dot(first, qs[:, :DH], 1, 1)
        two = dot(second, qs[:, DH:], 1, 1)
        s_full[0] = full
        key = lax.broadcasted_iota(jnp.int32, (RUN, ROWS), 0)
        row = lax.rem(lax.broadcasted_iota(jnp.int32, (RUN, ROWS), 1), RUN)
        tops = [top[0], jnp.maximum(top[1], fold(full, jnp.max))]
        for r in range(x_count):
            away = gap(own, r)
            for s, (tile, sign) in enumerate(((one, 1), (two, -1))):
                masked = jnp.where(key - row <= sign * away, tile[run(r)], NEG_FILL)
                s_mix[s, run(r), :] = masked
                tops[s] = jnp.maximum(tops[s], fold(masked, jnp.max))
        top[0], top[1] = tops

    def part(s):
        return slice(s * DH, (s + 1) * DH)

    def renew(batch):
        for s in range(2):
            highest = jnp.max(top[s], axis=0, keepdims=True)
            factor = jnp.exp2((peak[s, 0:1, :] - highest) * (SCALE * LOG2E))
            total[s] = total[s] * factor
            acc_out[part(s), :] = acc_out[part(s), :] * factor
            peak[s] = jnp.broadcast_to(highest, (8, ROWS))
            marks[batch, s] = jnp.broadcast_to(highest, (8, ROWS))

    def weigh(slot, group):
        highs = [peak[s] * (SCALE * LOG2E) for s in range(2)]
        full = jnp.exp2(s_full[slot] * (SCALE * LOG2E) - highs[1][0:1])
        totals = [total[0], total[1] + fold(full, jnp.sum)]
        full = full.astype(BF16)
        e_full[group] = full
        for r in range(x_count):
            is_early = early(group, r, (8, ROWS))
            high = jnp.where(is_early, highs[0], highs[1])[0:1]
            e = jnp.exp2(s_mix[slot, run(r), :] * (SCALE * LOG2E) - high)
            e_mix[group, run(r), :] = e.astype(BF16)
            summed = fold(e, jnp.sum)
            totals[0] = totals[0] + jnp.where(is_early, summed, 0.0)
            totals[1] = totals[1] + jnp.where(is_early, 0.0, summed)
        total[0], total[1] = totals
        acc_out[...] = acc_out[...] + dot(vm_t[slot], e_mix[group], 1, 0)
        acc_out[DH:, :] = acc_out[DH:, :] + dot(kv[0, group, :, DH:].T, full, 1, 0)

    def weigh_own():
        full = jnp.exp2((s_full[0] - peak[1, 0:1, :]) * (SCALE * LOG2E))
        one = jnp.exp2((s_mix[0] - peak[0, 0:1, :]) * (SCALE * LOG2E))
        two = jnp.exp2((s_mix[1] - peak[1, 0:1, :]) * (SCALE * LOG2E))
        total[0] = total[0] + fold(one, jnp.sum)
        total[1] = total[1] + fold(full, jnp.sum) + fold(two, jnp.sum)
        e_full[own] = full.astype(BF16)
        e_own[0] = one.astype(BF16)
        e_own[1] = two.astype(BF16)
        first, second = kv[0, own, :, DH:].T, kv[1, own, :, DH:].T
        acc_out[:DH, :] = acc_out[:DH, :] + dot(first, e_own[0], 1, 0)
        acc_out[DH:, :] = (
            acc_out[DH:, :] + dot(first, e_full[own], 1, 0) + dot(second, e_own[1], 1, 0)
        )

    def forward(batch, count, group_of):
        def first(j, carry):
            score(j, group_of(j))
            return carry

        def then(j, carry):
            weigh(j, group_of(j))
            return carry

        lax.fori_loop(0, count, first, 0)
        renew(batch)
        lax.fori_loop(0, count, then, 0)

    a_first = beside(kv.at[0, own, mine, :], kv.at[0, own, mine, :], ga[0], ga[1])
    b_moves = [move_b(way, 0, own) for way in range(2)]
    spreads = [spread(0, own)]
    arrive(a_first)
    a_moves = [move_a(way, 0, own) for way in range(2)]
    cross(0, 0, own)
    arrive(q_moves)
    for s in range(2):
        for h in range(RATIO):
            cols = slice(h * DH, (h + 1) * DH)
            qs[run(h), part(s)] = q_got[run(s), cols]
            dos[run(h), part(s)] = do_ref[run(s), cols]
    top[...] = jnp.full(top.shape, NEG_FILL, F32)
    peak[...] = jnp.full(peak.shape, NEG_FILL, F32)
    total[...] = jnp.zeros(total.shape, F32)
    acc_out[...] = jnp.zeros(acc_out.shape, F32)
    acc_dq[...] = jnp.zeros(acc_dq.shape, F32)
    finish(spreads)
    score_own()
    renew(0)
    weigh_own()

    def both(by):
        return lambda j: at.group(
            at.z_off(by * (2 * lax.rem(j, 2) - 1)), lax.rem(at.core + lax.div(j, 2), 2)
        )

    def crossed(indices):
        for i in indices:
            for half in range(2):
                crosses[half, i].wait_recv()

    for step in range(far):
        groups = [at.group(at.z_off((2 * way - 1) * (step + 1)), at.core) for way in range(2)]
        last = step == far - 1
        spreads = []
        arrive(b_moves)
        if last:
            spreads.append(spread(2 * far - 1, groups[0]))
        else:
            b_moves = [move_b(way, step + 1, groups[way]) for way in range(2)]
            spreads = [spread(2 * step + 1 + way, groups[way]) for way in range(2)]
        if last:
            arrive(a_moves)
            cross(0, 2 * far - 1, groups[0])
        else:
            for way in range(2):
                a_moves[way].wait_recv()
                a_moves[way] = move_a(way, step + 1, groups[way])
                cross(0, 2 * step + 1 + way, groups[way])
        if step == 0:
            crossed([0])
            forward(1, 1, lambda j: at.group(at.z, 1 - at.core))
        else:
            crossed([2 * step - 1, 2 * step])
            forward(1 + step, 4, both(step))
        finish(spreads)
    crossed([2 * far - 1])
    forward(1 + far, 2, lambda j: at.group(at.z_off(far), lax.rem(at.core + j, 2)))

    for s in range(2):
        inv = 1.0 / jnp.sum(total[s], axis=0, keepdims=True)
        out = (acc_out[part(s), :] * inv).astype(BF16).astype(F32)
        d_rows = dos[:, part(s)].astype(F32)
        q_part = qs[:, part(s)].astype(F32) * SCALE
        delta[s] = jnp.broadcast_to(jnp.sum(out * d_rows.T, axis=0, keepdims=True), (8, ROWS))
        total[s] = jnp.broadcast_to(inv, (8, ROWS))
        for batch in range(far + 2):
            factor = jnp.exp2((marks[batch, s] - peak[s]) * (SCALE * LOG2E))
            marks[batch, s] = factor
            by_row = jnp.broadcast_to(factor[0:1] * inv, (DH, ROWS)).T
            dod[batch, :, part(s)] = (d_rows * by_row).astype(BF16)
            qd[batch, :, part(s)] = (q_part * by_row).astype(BF16)
        out = out.T.astype(BF16)
        for h in range(RATIO):
            out_ref[run(s), h * DH : (h + 1) * DH] = out[run(h)]

    def backward(group, batch, who, i):
        full, mix = e_full[group], e_mix[group]
        ds_full = (full.astype(F32) * (dp_full[group] - delta[1, 0:1, :])).astype(BF16)
        ds_mix = []
        for r in range(x_count):
            shift = jnp.where(early(group, r, (8, ROWS)), delta[0], delta[1])[0:1]
            e = e_mix[group, run(r), :].astype(F32)
            ds_mix.append((e * (dp_mix[group, run(r), :] - shift)).astype(BF16))
        ds_mix = jnp.concatenate(ds_mix, axis=0)
        for cols, left, right, scaled in (
            (slice(0, DH), ds_full, ds_mix, qd),
            (slice(DH, 2 * DH), full, mix, dod),
        ):
            whole = dot(left, scaled[batch, :, DH:], 1, 0)
            mixed = dot(right, scaled[batch], 1, 0)
            for r in range(x_count):
                is_early = early(group, r, (RUN, DH))
                first = whole[run(r)] + jnp.where(is_early, mixed[run(r), :DH], 0.0)
                second = jnp.where(is_early, 0.0, mixed[run(r), DH:])
                parts[who, 0, i, run(r), cols] = first.astype(BF16)
                parts[who, 1, i, run(r), cols] = second.astype(BF16)
        grad = dot(km_t[group], ds_mix, 1, 0)
        late = grad[DH:] + dot(ka_t[group], ds_full, 1, 0)
        acc_dq[:DH, :] = acc_dq[:DH, :] + marks[batch, 0, 0:1, :] * grad[:DH]
        acc_dq[DH:, :] = acc_dq[DH:, :] + marks[batch, 1, 0:1, :] * late

    def backward_own(i):
        first, second = kv[0, own], kv[1, own]
        d_one, d_two = delta[0, 0:1, :], delta[1, 0:1, :]

        def ds(e, values, s, shift):
            dp = dot(values[:, DH:], dos[:, part(s)], 1, 1)
            return (e.astype(F32) * (dp - shift)).astype(BF16)

        ds_full = ds(e_full[own], first, 1, d_two)
        ds_one = ds(e_own[0], first, 0, d_one)
        ds_two = ds(e_own[1], second, 1, d_two)
        for cols, full, one, two, scaled in (
            (slice(0, DH), ds_full, ds_one, ds_two, qd),
            (slice(DH, 2 * DH), e_full[own], e_own[0], e_own[1], dod),
        ):
            parts[1, 0, i, :, cols] = (
                dot(full, scaled[0, :, DH:], 1, 0) + dot(one, scaled[0, :, :DH], 1, 0)
            ).astype(BF16)
            parts[1, 1, i, :, cols] = dot(two, scaled[0, :, DH:], 1, 0).astype(BF16)
        first, second = first[:, :DH].T, second[:, :DH].T
        acc_dq[:DH, :] = acc_dq[:DH, :] + marks[0, 0, 0:1, :] * dot(first, ds_one, 1, 0)
        acc_dq[DH:, :] = acc_dq[DH:, :] + marks[0, 1, 0:1, :] * (
            dot(first, ds_full, 1, 0) + dot(second, ds_two, 1, 0)
        )

    hand_over = {}

    def give(i):
        for half in (1, 0):
            send, recv = (sb, sa)[1 - half][4:]
            copy = push(
                parts.at[0, half, i],
                other.at[half, i],
                send.at[i],
                recv.at[i],
                at.device(core=1 - at.core),
            )
            sent.append(copy)
            hand_over[half, i] = copy

    def pair(half, i):
        hand_over[half, i].wait_recv()
        return parts[1, half, i].astype(F32) + other[half, i].astype(F32)

    def across(src, dst, send, recv):
        copies = []
        for d in range(1, at.xs):
            x = at.x_off(d)
            place = pl.ds(pl.multiple_of(x * rows, rows), rows)
            copies.append(
                push(src.at[place, :], dst.at[d - 1], send.at[d - 1], recv.at[d - 1], at.device(x=x))
            )
        sent.extend(copies)
        return copies

    def spread_b(i):
        both_cores = pair(1, i)
        keep[i] = both_cores
        xb_out[i] = both_cores.astype(BF16)
        return across(xb_out.at[i], xb_in.at[i], sb[0].at[i], sb[1].at[i])

    def collect(copies, kept, arrived):
        summed = kept[mine, :]
        for d in range(1, at.xs):
            copies[d - 1].wait_recv()
            summed = summed + arrived[d - 1].astype(F32)
        return summed

    def collect_b(i):
        return collect(b_spreads[i], keep.at[i], xb_in.at[i])

    def half_of(way, length):
        return slice(way * (length // 2), (way + 1) * (length // 2))

    def along(out, into, sems, way, step):
        length = out.shape[2]
        place = pl.ds(way * (length // 2), length // 2) if step == 0 else pl.ds(0, length)
        copy = push(
            out.at[way, step, place, :],
            into.at[way, step, place, :],
            sems[2].at[way, step],
            sems[3].at[way, step],
            towards(way),
        )
        sent.append(copy)
        return copy

    def begin(summed, out, into, sems):
        moves = []
        for way in range(2):
            place = half_of(way, out.shape[2])
            out[way, 0, place, :] = summed[place].astype(BF16)
            moves.append(along(out, into, sems, way, 0))
        return moves

    def go_on(moves, way, step, summed, out, into, sems):
        moves[way].wait_recv()
        if step == 1:
            near, rest = half_of(way, out.shape[2]), half_of(1 - way, out.shape[2])
            out[way, 1, near, :] = (summed[near] + into[way, 0, near, :].astype(F32)).astype(BF16)
            out[way, 1, rest, :] = summed[rest].astype(BF16)
        else:
            out[way, step] = (summed + into[way, step - 1].astype(F32)).astype(BF16)
        moves[way] = along(out, into, sems, way, step)

    def end(moves, summed, into):
        for way in range(2):
            moves[way].wait_recv()
            summed = summed + into[way, far - 1].astype(F32)
        return summed

    def back(who, step):
        core = lax.rem(at.core + 1 + who, 2)

        def one_way(way, carry):
            offset = (far - step) * (1 - 2 * way)
            group = at.group(at.z_off(offset), core)
            backward(group, 1 + far - step, who, 2 * step - 1 + way)
            return carry

        lax.fori_loop(0, 2, one_way, 0)

    a_refs = (za_out, za_in, sa)
    b_refs = (zb_out, zb_in, sb)
    backward(at.group(at.z_off(far), 1 - at.core), 1 + far, 0, 0)
    give(0)
    backward(at.group(at.z_off(far), at.core), 1 + far, 1, 0)
    b_spreads = {0: spread_b(0)}
    a_moves = begin(pair(0, 0), *a_refs)
    b_moves = None
    for step in range(1, far):
        back(0, step)
        give(2 * step - 1)
        give(2 * step)
        back(1, step)
        for way in range(2):
            b_spreads[2 * step - 1 + way] = spread_b(2 * step - 1 + way)
        for way in range(2):
            go_on(a_moves, way, step, pair(0, 2 * step - 1 + way), *a_refs)
        if step == 1:
            b_moves = begin(collect_b(0), *b_refs)
        else:
            for way in range(2):
                go_on(b_moves, way, step - 1, collect_b(2 * step - 3 + way), *b_refs)
    backward(at.group(at.z, 1 - at.core), 1, 0, at.zs - 1)
    give(at.zs - 1)
    for way in range(2):
        go_on(b_moves, way, far - 1, collect_b(2 * far - 3 + way), *b_refs)
    backward_own(at.zs - 1)
    b_spreads[at.zs - 1] = spread_b(at.zs - 1)
    mine_a = end(a_moves, pair(0, at.zs - 1), za_in)
    other_a = keep.at[0]
    other_a[...] = mine_a
    xa_out[...] = mine_a.astype(BF16)
    last_a = across(xa_out, xa_in, sa[0], sa[1])
    for s in range(2):
        grad = (acc_dq[part(s), :] * (total[s, 0:1, :] * SCALE)).T.astype(BF16)
        for h in range(RATIO):
            dq_ref[run(s), h * DH : (h + 1) * DH] = grad[run(h)]
    second = end(b_moves, collect_b(at.zs - 1), zb_in)
    gk_ref[rows:, :] = second[:, :DH].astype(BF16)
    gv_ref[rows:, :] = second[:, DH:].astype(BF16)
    first = collect(last_a, keep.at[0], xa_in)
    gk_ref[:rows, :] = first[:, :DH].astype(BF16)
    gv_ref[:rows, :] = first[:, DH:].astype(BF16)
    for copy in sent:
        copy.wait_send()


def layer(x_count, positions, q_rows, k_rows, v_rows, dout):
    heads = lax.axis_size("head")
    rows = heads * q_rows.shape[0]
    width = q_rows.shape[1] // heads
    zs = 2 * (lax.axis_size("outer") // x_count)
    far = zs // 2
    run = rows // 2
    size = x_count * run
    batches = far + 2
    kv_width = 2 * DH
    dma = pltpu.SemaphoreType.DMA
    vmem = pl.BlockSpec(memory_space=pltpu.VMEM)
    sems = [(3, heads - 1), (3, heads - 1)]
    for x_dims in ((x_count - 1,), (zs, x_count - 1)) * 2:
        sems += [x_dims, x_dims, (2, far), (2, far), (zs,), (zs,)]
    buffers = [
        ((rows, width), BF16),
        ((rows, kv_width), BF16),
        ((2, 2 * zs, size, kv_width), BF16),
        ((ROWS, 2 * DH), BF16),
        ((ROWS, 2 * DH), BF16),
        ((4, size, ROWS), F32),
        ((4, size, ROWS), F32),
        ((2 * zs, size, ROWS), BF16),
        ((2 * zs, size, ROWS), BF16),
        ((2, size, ROWS), BF16),
        ((2 * zs, size, kv_width), BF16),
        ((size, kv_width), BF16),
        ((2 * zs, kv_width, size), BF16),
        ((2 * zs, DH, size), BF16),
        ((2 * zs, size, ROWS), F32),
        ((2 * zs, size, ROWS), F32),
        ((4, kv_width, size), BF16),
        ((2, 8, ROWS), F32),
        ((2, 8, ROWS), F32),
        ((2, 8, ROWS), F32),
        ((batches, 2, 8, ROWS), F32),
        ((2 * DH, ROWS), F32),
        ((2 * DH, ROWS), F32),
        ((batches, ROWS, 2 * DH), BF16),
        ((batches, ROWS, 2 * DH), BF16),
        ((2, 8, ROWS), F32),
        ((2, 2, zs, size, kv_width), BF16),
        ((2, zs, size, kv_width), BF16),
        ((2, far, size, kv_width), BF16),
        ((2, far, size, kv_width), BF16),
        ((2, far, run, kv_width), BF16),
        ((2, far, run, kv_width), BF16),
        ((x_count - 1, run, kv_width), BF16),
        ((size, kv_width), BF16),
        ((zs, x_count - 1, run, kv_width), BF16),
        ((zs, size, kv_width), BF16),
        ((zs, size, kv_width), F32),
    ]
    return pl.pallas_call(
        functools.partial(layer_kernel, x_count),
        out_shape=(jax.ShapeDtypeStruct((rows, width), BF16),) * 2
        + (jax.ShapeDtypeStruct((rows, DH), BF16),) * 2,
        in_specs=[pl.BlockSpec(memory_space=pltpu.SMEM)] + [vmem] * 4,
        out_specs=(vmem,) * 4,
        scratch_shapes=[pltpu.VMEM(dims, kind) for dims, kind in buffers]
        + [dma(dims) for dims in sems],
        compiler_params=pltpu.CompilerParams(
            collective_id=0, has_side_effects=True, vmem_limit_bytes=56 * 1024 * 1024
        ),
    )(positions, q_rows, k_rows, v_rows, dout)


def hand_in_kernel(*refs):
    half = len(refs) // 2
    for src, dst in zip(refs[:half], refs[half:]):
        dst[...] = src[...]


def hand_in(*results):
    vmem = pl.BlockSpec(memory_space=pltpu.VMEM)
    return pl.pallas_call(
        hand_in_kernel,
        out_shape=tuple(jax.ShapeDtypeStruct(x.shape, x.dtype) for x in results),
        in_specs=[vmem] * len(results),
        out_specs=(vmem,) * len(results),
    )(*results)


def shards(q_rows, k_rows, v_rows, dout, positions):
    return hand_in(*layer(CHIPS_X, positions, q_rows, k_rows, v_rows, dout))


def solution(mesh):
    return jax.shard_map(
        shards,
        mesh=mesh,
        in_specs=(
            P(("inner", "outer", "head"), None),
            P(("inner", "outer", "head"), None),
            P(("inner", "outer", "head"), None),
            P(("inner", "outer"), "head"),
            P(),
        ),
        out_specs=(
            P(("inner", "outer"), "head"),
            P(("inner", "outer"), "head"),
            P(("inner", "outer"), "head"),
            P(("inner", "outer"), "head"),
        ),
        check_vma=False,
    )
```

```python
import functools

import jax
import jax.numpy as jnp
from jax import lax
from jax.experimental import pallas as pl
from jax.experimental.pallas import tpu as pltpu
from jax.sharding import PartitionSpec as P

QH = 32
KVH = 8
DH = 128
RUN = 64
BLOCKS = 64
CHIPS_X = 4
RATIO = QH // KVH
ROWS = RATIO * RUN
CHUNK = 256
RUNS_CHUNK = CHUNK // RUN
CHUNKS = 2 * BLOCKS // RUNS_CHUNK
ITEMS = CHUNKS + 1
LOG2E = 1.4426950408889634
SCALE = DH**-0.5
NEG_FILL = -1e30
F32 = jnp.float32
BF16 = jnp.bfloat16


def dot(a, b, ca, cb):
    return lax.dot_general(a, b, (((ca,), (cb,)), ((), ())), preferred_element_type=F32)


MESH = pl.DeviceIdType.MESH


class Plane:
    def __init__(self, x_count):
        inner, outer = lax.axis_index("inner"), lax.axis_index("outer")
        self.xs = x_count
        self.z_pairs = lax.axis_size("outer") // x_count
        self.zs = 2 * self.z_pairs
        self.x = lax.rem(outer, x_count)
        self.core = lax.rem(inner, 2)
        self.z = 2 * lax.div(outer, x_count) + lax.div(inner, 2)

    def z_off(self, by):
        return lax.rem(self.z + by + self.zs, self.zs)

    def x_off(self, by):
        return lax.rem(self.x + by + self.xs, self.xs)

    def group(self, z, core):
        return (2 * lax.rem(z, 2) + core) * self.z_pairs + lax.div(z, 2)

    def device(self, z=None, core=None, x=None):
        z = self.z if z is None else z
        core = self.core if core is None else core
        x = self.x if x is None else x
        return {"inner": 2 * lax.rem(z, 2) + core, "outer": lax.div(z, 2) * self.xs + x}

    def partners(self):
        found = [self.device(core=1 - self.core)]
        found += [self.device(z=self.z_off(1)), self.device(z=self.z_off(-1))]
        found += [self.device(x=self.x_off(d)) for d in range(1, self.xs)]
        return found

    def greet(self, heads=1):
        head = lax.axis_index("head")
        partners = [{"head": lax.rem(head + d, heads)} for d in range(1, heads)]
        partners += self.partners()
        barrier = pltpu.get_barrier_semaphore()
        for device in partners:
            pl.semaphore_signal(barrier, inc=1, device_id=device, device_id_type=MESH)
        pl.semaphore_wait(barrier, len(partners))


def push(src, dst, send_sem, recv_sem, device):
    copy = pltpu.make_async_remote_copy(
        src_ref=src,
        dst_ref=dst,
        send_sem=send_sem,
        recv_sem=recv_sem,
        device_id=device,
        device_id_type=MESH,
    )
    copy.start()
    return copy


def layer_kernel(
    x_count,
    pos_ref,
    q_ref,
    k_ref,
    v_ref,
    do_ref,
    out_ref,
    dq_ref,
    gk_ref,
    gv_ref,
    q_got,
    block,
    kv,
    qs,
    dos,
    s_full,
    s_mix,
    e_full,
    e_mix,
    e_own,
    km,
    vm,
    km_t,
    ka_t,
    dp_full,
    dp_mix,
    vm_t,
    top,
    peak,
    total,
    marks,
    acc_out,
    acc_dq,
    qd,
    dod,
    delta,
    parts,
    other,
    za_in,
    za_out,
    zb_in,
    zb_out,
    xa_in,
    xa_out,
    xb_in,
    xb_out,
    keep,
    y_send,
    y_recv,
    *sems,
):
    at = Plane(x_count)
    heads = lax.axis_size("head")
    far = at.zs // 2
    tokens = q_ref.shape[0]
    width = q_ref.shape[1] // heads
    rows = block.shape[0] // 2
    size = x_count * rows
    ga, gb, sa, sb = (sems[6 * i : 6 * i + 6] for i in range(4))
    at.greet(heads)

    head = lax.axis_index("head")
    here = pl.ds(pl.multiple_of(head * tokens, tokens), tokens)
    q_moves, kv_moves = [], []
    for d in range(1, heads):
        peer = lax.rem(head + d, heads)
        cols = pl.ds(pl.multiple_of(peer * DH, DH), DH)
        for i, src in enumerate((k_ref, v_ref)):
            kv_moves.append(
                push(
                    src.at[:, cols],
                    block.at[here, pl.ds(i * DH, DH)],
                    y_send.at[i, d - 1],
                    y_recv.at[i, d - 1],
                    {"head": peer},
                )
            )
    for d in range(1, heads):
        peer = lax.rem(head + d, heads)
        cols = pl.ds(pl.multiple_of(peer * width, width), width)
        q_moves.append(
            push(
                q_ref.at[:, cols],
                q_got.at[here, :],
                y_send.at[2, d - 1],
                y_recv.at[2, d - 1],
                {"head": peer},
            )
        )
    cols = pl.ds(pl.multiple_of(head * DH, DH), DH)
    block[here, :DH] = k_ref[:, cols]
    block[here, DH:] = v_ref[:, cols]
    q_got[here, :] = q_ref[:, pl.ds(pl.multiple_of(head * width, width), width)]
    for copy in kv_moves:
        copy.wait_recv()
    sent = kv_moves + q_moves

    mine = pl.ds(pl.multiple_of(at.x * rows, rows), rows)
    own = at.group(at.z, at.core)
    kv[0, own, mine, :] = block[:rows, :]
    kv[1, own, mine, :] = block[rows:, :]

    def towards(way):
        return at.device(z=at.z_off(1 - 2 * way))

    def beside(src, dst, send, recv):
        copies = [
            push(src, dst, send.at[d - 1], recv.at[d - 1], at.device(x=at.x_off(d)))
            for d in range(1, at.xs)
        ]
        sent.extend(copies)
        return copies

    def arrive(copies):
        for copy in copies:
            copy.wait_recv()

    def move_a(way, step, k, group):
        if step == far - 1 and k != way:
            return None
        part = kv.at[0, group, pl.ds(k * (size // 2), size // 2), :]
        copy = push(part, part, ga[2].at[way, step, k], ga[3].at[way, step, k], towards(way))
        sent.append(copy)
        return copy

    def move_b(way, step, group):
        place = mine
        if step == far - 1:
            place = pl.ds(pl.multiple_of(at.x * rows + way * (rows // 2), rows // 2), rows // 2)
        part = kv.at[1, group, place, :]
        copy = push(part, part, gb[2].at[way, step], gb[3].at[way, step], towards(way))
        sent.append(copy)
        return copy

    crosses = {}

    def cross(half, i, group):
        whole = kv.at[half, group]
        send, recv = (gb, ga)[1 - half][4:]
        copy = push(whole, whole, send.at[i], recv.at[i], at.device(core=1 - at.core))
        sent.append(copy)
        crosses[half, i] = copy

    def one(src, dst, send, recv, device):
        copy = push(src, dst, send, recv, device)
        sent.append(copy)
        return copy

    pair_start = lax.div(at.x, 2) * (2 * rows)
    mine_pair = pl.ds(pl.multiple_of(pair_start, 2 * rows), 2 * rows)
    facing_pair = pl.ds(pl.multiple_of(2 * rows - pair_start, 2 * rows), 2 * rows)
    beside_me = at.device(x=at.x + 1 - 2 * lax.rem(at.x, 2))
    facing_me = at.device(x=at.xs - 1 - at.x)

    def spread(i, group):
        part = kv.at[1, group, mine, :]
        return i, group, one(part, part, gb[0].at[i, 0], gb[1].at[i, 0], beside_me)

    def widen(spreads):
        wider = []
        for i, group, copy in spreads:
            copy.wait_recv()
            part = kv.at[1, group, mine_pair, :]
            copy = one(part, part, gb[0].at[i, 1], gb[1].at[i, 1], facing_me)
            wider.append((i, group, copy))
        return wider

    def finish(spreads):
        for i, group, copy in spreads:
            copy.wait_recv()
            cross(1, i, group)

    def fold(x, op):
        return op(x.reshape(x.shape[0] // 8, 8, ROWS), axis=0)

    def gap(group, r):
        mine_first = pos_ref[(x_count * own + at.x) * 2 * rows]
        return mine_first - pos_ref[(x_count * group + r) * 2 * rows]

    def early(group, r, shape=(RUN, ROWS)):
        return jnp.full(shape, gap(group, r), jnp.int32) >= 0

    def run(r):
        return slice(r * RUN, (r + 1) * RUN)

    def prepare(group):
        first, second = kv[0, group], kv[1, group]
        for r in range(x_count):
            is_early = early(group, r, (RUN, 2 * DH))
            left = jnp.where(is_early, first[run(r)].astype(F32), 0.0).astype(BF16)
            right = jnp.where(is_early, 0.0, second[run(r)].astype(F32)).astype(BF16)
            km[group, run(r), :] = jnp.concatenate([left[:, :DH], right[:, :DH]], axis=1)
            vm[run(r), :] = jnp.concatenate([left[:, DH:], right[:, DH:]], axis=1)
        km_t[group] = km[group].T
        ka_t[group] = first[:, :DH].T
        dp_full[group] = dot(first[:, DH:], dos[:, DH:], 1, 1)
        dp_mix[group] = dot(vm[...], dos[...], 1, 1)
        return vm[...].T

    def score(slot, group):
        full = dot(kv[0, group, :, :DH], qs[:, DH:], 1, 1)
        vm_t[slot] = prepare(group)
        mix = dot(km[group], qs[...], 1, 1)
        s_full[slot] = full
        s_mix[slot] = mix
        tops = [top[0], jnp.maximum(top[1], fold(full, jnp.max))]
        for r in range(x_count):
            is_early = early(group, r, (8, ROWS))
            highest = fold(mix[run(r)], jnp.max)
            tops[0] = jnp.maximum(tops[0], jnp.where(is_early, highest, NEG_FILL))
            tops[1] = jnp.maximum(tops[1], jnp.where(is_early, NEG_FILL, highest))
        top[0], top[1] = tops

    def score_own():
        first, second = kv[0, own, :, :DH], kv[1, own, :, :DH]
        full = dot(first, qs[:, DH:], 1, 1)
        one = dot(first, qs[:, :DH], 1, 1)
        two = dot(second, qs[:, DH:], 1, 1)
        s_full[0] = full
        key = lax.broadcasted_iota(jnp.int32, (RUN, ROWS), 0)
        row = lax.rem(lax.broadcasted_iota(jnp.int32, (RUN, ROWS), 1), RUN)
        tops = [top[0], jnp.maximum(top[1], fold(full, jnp.max))]
        for r in range(x_count):
            away = gap(own, r)
            for s, (tile, sign) in enumerate(((one, 1), (two, -1))):
                masked = jnp.where(key - row <= sign * away, tile[run(r)], NEG_FILL)
                s_mix[s, run(r), :] = masked
                tops[s] = jnp.maximum(tops[s], fold(masked, jnp.max))
        top[0], top[1] = tops

    def part(s):
        return slice(s * DH, (s + 1) * DH)

    def renew(batch):
        for s in range(2):
            highest = jnp.max(top[s], axis=0, keepdims=True)
            factor = jnp.exp2((peak[s, 0:1, :] - highest) * (SCALE * LOG2E))
            total[s] = total[s] * factor
            acc_out[part(s), :] = acc_out[part(s), :] * factor
            peak[s] = jnp.broadcast_to(highest, (8, ROWS))
            marks[batch, s] = jnp.broadcast_to(highest, (8, ROWS))

    def weigh(slot, group):
        highs = [peak[s] * (SCALE * LOG2E) for s in range(2)]
        full = jnp.exp2(s_full[slot] * (SCALE * LOG2E) - highs[1][0:1])
        totals = [total[0], total[1] + fold(full, jnp.sum)]
        full = full.astype(BF16)
        e_full[group] = full
        for r in range(x_count):
            is_early = early(group, r, (8, ROWS))
            high = jnp.where(is_early, highs[0], highs[1])[0:1]
            e = jnp.exp2(s_mix[slot, run(r), :] * (SCALE * LOG2E) - high)
            e_mix[group, run(r), :] = e.astype(BF16)
            summed = fold(e, jnp.sum)
            totals[0] = totals[0] + jnp.where(is_early, summed, 0.0)
            totals[1] = totals[1] + jnp.where(is_early, 0.0, summed)
        total[0], total[1] = totals
        acc_out[...] = acc_out[...] + dot(vm_t[slot], e_mix[group], 1, 0)
        acc_out[DH:, :] = acc_out[DH:, :] + dot(kv[0, group, :, DH:].T, full, 1, 0)

    def weigh_own():
        full = jnp.exp2((s_full[0] - peak[1, 0:1, :]) * (SCALE * LOG2E))
        one = jnp.exp2((s_mix[0] - peak[0, 0:1, :]) * (SCALE * LOG2E))
        two = jnp.exp2((s_mix[1] - peak[1, 0:1, :]) * (SCALE * LOG2E))
        total[0] = total[0] + fold(one, jnp.sum)
        total[1] = total[1] + fold(full, jnp.sum) + fold(two, jnp.sum)
        e_full[own] = full.astype(BF16)
        e_own[0] = one.astype(BF16)
        e_own[1] = two.astype(BF16)
        first, second = kv[0, own, :, DH:].T, kv[1, own, :, DH:].T
        acc_out[:DH, :] = acc_out[:DH, :] + dot(first, e_own[0], 1, 0)
        acc_out[DH:, :] = (
            acc_out[DH:, :] + dot(first, e_full[own], 1, 0) + dot(second, e_own[1], 1, 0)
        )

    def forward(batch, count, group_of):
        def first(j, carry):
            score(j, group_of(j))
            return carry

        def then(j, carry):
            weigh(j, group_of(j))
            return carry

        lax.fori_loop(0, count, first, 0)
        renew(batch)
        lax.fori_loop(0, count, then, 0)

    a_first = beside(kv.at[0, own, mine, :], kv.at[0, own, mine, :], ga[0], ga[1])
    b_moves = [move_b(way, 0, own) for way in range(2)]
    spreads = [spread(0, own)]
    arrive(a_first)
    a_moves = [[move_a(way, 0, k, own) for way in range(2)] for k in range(2)]
    cross(0, 0, own)
    spreads = widen(spreads)
    arrive(q_moves)
    for s in range(2):
        for h in range(RATIO):
            cols = slice(h * DH, (h + 1) * DH)
            qs[run(h), part(s)] = q_got[run(s), cols]
            dos[run(h), part(s)] = do_ref[run(s), cols]
    top[...] = jnp.full(top.shape, NEG_FILL, F32)
    peak[...] = jnp.full(peak.shape, NEG_FILL, F32)
    total[...] = jnp.zeros(total.shape, F32)
    acc_out[...] = jnp.zeros(acc_out.shape, F32)
    acc_dq[...] = jnp.zeros(acc_dq.shape, F32)
    finish(spreads)
    score_own()
    renew(0)
    weigh_own()

    def both(by):
        return lambda j: at.group(
            at.z_off(by * (2 * lax.rem(j, 2) - 1)), lax.rem(at.core + lax.div(j, 2), 2)
        )

    def crossed(indices):
        for i in indices:
            for half in range(2):
                crosses[half, i].wait_recv()

    for step in range(far):
        groups = [at.group(at.z_off((2 * way - 1) * (step + 1)), at.core) for way in range(2)]
        last = step == far - 1
        spreads = []
        arrive(b_moves)
        if last:
            spreads.append(spread(2 * far - 1, groups[0]))
        else:
            b_moves = [move_b(way, step + 1, groups[way]) for way in range(2)]
            spreads = [spread(2 * step + 1 + way, groups[way]) for way in range(2)]
        for k in range(2):
            for way in range(2):
                if a_moves[k][way] is not None:
                    a_moves[k][way].wait_recv()
                if not last:
                    a_moves[k][way] = move_a(way, step + 1, k, groups[way])
        if last:
            cross(0, 2 * far - 1, groups[0])
        else:
            for way in range(2):
                cross(0, 2 * step + 1 + way, groups[way])
        spreads = widen(spreads)
        if step == 0:
            crossed([0])
            forward(1, 1, lambda j: at.group(at.z, 1 - at.core))
        else:
            crossed([2 * step - 1, 2 * step])
            forward(1 + step, 4, both(step))
        finish(spreads)
    crossed([2 * far - 1])
    forward(1 + far, 2, lambda j: at.group(at.z_off(far), lax.rem(at.core + j, 2)))

    for s in range(2):
        inv = 1.0 / jnp.sum(total[s], axis=0, keepdims=True)
        out = (acc_out[part(s), :] * inv).astype(BF16).astype(F32)
        d_rows = dos[:, part(s)].astype(F32)
        q_part = qs[:, part(s)].astype(F32) * SCALE
        delta[s] = jnp.broadcast_to(jnp.sum(out * d_rows.T, axis=0, keepdims=True), (8, ROWS))
        total[s] = jnp.broadcast_to(inv, (8, ROWS))
        for batch in range(far + 2):
            factor = jnp.exp2((marks[batch, s] - peak[s]) * (SCALE * LOG2E))
            marks[batch, s] = factor
            by_row = jnp.broadcast_to(factor[0:1] * inv, (DH, ROWS)).T
            dod[batch, :, part(s)] = (d_rows * by_row).astype(BF16)
            qd[batch, :, part(s)] = (q_part * by_row).astype(BF16)
        out = out.T.astype(BF16)
        for h in range(RATIO):
            out_ref[run(s), h * DH : (h + 1) * DH] = out[run(h)]

    def backward(group, batch, who, i):
        full, mix = e_full[group], e_mix[group]
        ds_full = (full.astype(F32) * (dp_full[group] - delta[1, 0:1, :])).astype(BF16)
        ds_mix = []
        for r in range(x_count):
            shift = jnp.where(early(group, r, (8, ROWS)), delta[0], delta[1])[0:1]
            e = e_mix[group, run(r), :].astype(F32)
            ds_mix.append((e * (dp_mix[group, run(r), :] - shift)).astype(BF16))
        ds_mix = jnp.concatenate(ds_mix, axis=0)
        for cols, left, right, scaled in (
            (slice(0, DH), ds_full, ds_mix, qd),
            (slice(DH, 2 * DH), full, mix, dod),
        ):
            whole = dot(left, scaled[batch, :, DH:], 1, 0)
            mixed = dot(right, scaled[batch], 1, 0)
            for r in range(x_count):
                is_early = early(group, r, (RUN, DH))
                first = whole[run(r)] + jnp.where(is_early, mixed[run(r), :DH], 0.0)
                second = jnp.where(is_early, 0.0, mixed[run(r), DH:])
                parts[who, 0, i, run(r), cols] = first.astype(BF16)
                parts[who, 1, i, run(r), cols] = second.astype(BF16)
        grad = dot(km_t[group], ds_mix, 1, 0)
        late = grad[DH:] + dot(ka_t[group], ds_full, 1, 0)
        acc_dq[:DH, :] = acc_dq[:DH, :] + marks[batch, 0, 0:1, :] * grad[:DH]
        acc_dq[DH:, :] = acc_dq[DH:, :] + marks[batch, 1, 0:1, :] * late

    def backward_own(i):
        first, second = kv[0, own], kv[1, own]
        d_one, d_two = delta[0, 0:1, :], delta[1, 0:1, :]

        def ds(e, values, s, shift):
            dp = dot(values[:, DH:], dos[:, part(s)], 1, 1)
            return (e.astype(F32) * (dp - shift)).astype(BF16)

        ds_full = ds(e_full[own], first, 1, d_two)
        ds_one = ds(e_own[0], first, 0, d_one)
        ds_two = ds(e_own[1], second, 1, d_two)
        for cols, full, one, two, scaled in (
            (slice(0, DH), ds_full, ds_one, ds_two, qd),
            (slice(DH, 2 * DH), e_full[own], e_own[0], e_own[1], dod),
        ):
            parts[1, 0, i, :, cols] = (
                dot(full, scaled[0, :, DH:], 1, 0) + dot(one, scaled[0, :, :DH], 1, 0)
            ).astype(BF16)
            parts[1, 1, i, :, cols] = dot(two, scaled[0, :, DH:], 1, 0).astype(BF16)
        first, second = first[:, :DH].T, second[:, :DH].T
        acc_dq[:DH, :] = acc_dq[:DH, :] + marks[0, 0, 0:1, :] * dot(first, ds_one, 1, 0)
        acc_dq[DH:, :] = acc_dq[DH:, :] + marks[0, 1, 0:1, :] * (
            dot(first, ds_full, 1, 0) + dot(second, ds_two, 1, 0)
        )

    hand_over = {}

    def give(i):
        for half in (1, 0):
            send, recv = (sb, sa)[1 - half][4:]
            copy = push(
                parts.at[0, half, i],
                other.at[half, i],
                send.at[i],
                recv.at[i],
                at.device(core=1 - at.core),
            )
            sent.append(copy)
            hand_over[half, i] = copy

    def pair(half, i):
        hand_over[half, i].wait_recv()
        return parts[1, half, i].astype(F32) + other[half, i].astype(F32)

    def across(src, dst, send, recv):
        copies = []
        for d in range(1, at.xs):
            x = at.x_off(d)
            place = pl.ds(pl.multiple_of(x * rows, rows), rows)
            copies.append(
                push(src.at[place, :], dst.at[d - 1], send.at[d - 1], recv.at[d - 1], at.device(x=x))
            )
        sent.extend(copies)
        return copies

    def first_b(i):
        keep[i] = pair(1, i)
        xb_out[i, : 2 * rows, :] = keep[i, facing_pair, :].astype(BF16)
        b_copies[i] = one(
            xb_out.at[i, pl.ds(0, 2 * rows), :],
            xb_in.at[i, pl.ds(0, 2 * rows), :],
            sb[0].at[i, 0],
            sb[1].at[i, 0],
            facing_me,
        )

    def second_b(i):
        b_copies[i].wait_recv()
        summed = keep[i, mine_pair, :] + xb_in[i, : 2 * rows, :].astype(F32)
        keep[i, mine_pair, :] = summed
        xb_out[i, 2 * rows :, :] = summed.astype(BF16)
        theirs = 2 * rows + (1 - lax.rem(at.x, 2)) * rows
        b_copies[i] = one(
            xb_out.at[i, pl.ds(pl.multiple_of(theirs, rows), rows), :],
            xb_in.at[i, pl.ds(2 * rows, rows), :],
            sb[0].at[i, 1],
            sb[1].at[i, 1],
            beside_me,
        )

    b_copies = {}

    def collect(copies, kept, arrived):
        summed = kept[mine, :]
        for d in range(1, at.xs):
            copies[d - 1].wait_recv()
            summed = summed + arrived[d - 1].astype(F32)
        return summed

    def collect_b(i):
        b_copies[i].wait_recv()
        return keep[i, mine, :] + xb_in[i, 2 * rows : 3 * rows, :].astype(F32)

    def half_of(way, length):
        return slice(way * (length // 2), (way + 1) * (length // 2))

    def along(out, into, sems, way, step, k):
        length = out.shape[2]
        place = pl.ds(k * (length // 2), length // 2)
        return one(
            out.at[way, step, place, :],
            into.at[way, step, place, :],
            sems[2].at[way, step, k],
            sems[3].at[way, step, k],
            towards(way),
        )

    def begin(summed, out, into, sems):
        moves = [[None, None], [None, None]]
        for way in range(2):
            place = half_of(way, out.shape[2])
            out[way, 0, place, :] = summed[place].astype(BF16)
            moves[way][way] = along(out, into, sems, way, 0, way)
        return moves

    def go_on(moves, way, step, summed, out, into, sems):
        for k in (1 - way, way):
            place = half_of(k, out.shape[2])
            value = summed[place]
            if moves[way][k] is not None:
                moves[way][k].wait_recv()
                value = value + into[way, step - 1, place, :].astype(F32)
            out[way, step, place, :] = value.astype(BF16)
            moves[way][k] = along(out, into, sems, way, step, k)

    def end(moves, summed, into):
        for way in range(2):
            for k in range(2):
                moves[way][k].wait_recv()
            summed = summed + into[way, far - 1].astype(F32)
        return summed

    def back(who, step):
        core = lax.rem(at.core + 1 + who, 2)

        def one_way(way, carry):
            offset = (far - step) * (1 - 2 * way)
            group = at.group(at.z_off(offset), core)
            backward(group, 1 + far - step, who, 2 * step - 1 + way)
            return carry

        lax.fori_loop(0, 2, one_way, 0)

    a_refs = (za_out, za_in, sa)
    b_refs = (zb_out, zb_in, sb)
    backward(at.group(at.z_off(far), 1 - at.core), 1 + far, 0, 0)
    give(0)
    backward(at.group(at.z_off(far), at.core), 1 + far, 1, 0)
    first_b(0)
    a_moves = begin(pair(0, 0), *a_refs)
    b_moves = None
    for step in range(1, far):
        before = [0] if step == 1 else [2 * step - 3, 2 * step - 2]
        here = [2 * step - 1, 2 * step]
        back(0, step)
        for i in here:
            give(i)
        for i in before:
            second_b(i)
        back(1, step)
        for i in here:
            first_b(i)
        for way in range(2):
            go_on(a_moves, way, step, pair(0, here[way]), *a_refs)
        if step == 1:
            b_moves = begin(collect_b(0), *b_refs)
        else:
            for way in range(2):
                go_on(b_moves, way, step - 1, collect_b(before[way]), *b_refs)
    backward(at.group(at.z, 1 - at.core), 1, 0, at.zs - 1)
    give(at.zs - 1)
    for i in here:
        second_b(i)
    backward_own(at.zs - 1)
    first_b(at.zs - 1)
    for way in range(2):
        go_on(b_moves, way, far - 1, collect_b(here[way]), *b_refs)
    mine_a = end(a_moves, pair(0, at.zs - 1), za_in)
    keep[0] = mine_a
    xa_out[...] = mine_a.astype(BF16)
    last_a = across(xa_out, xa_in, sa[0], sa[1])
    second_b(at.zs - 1)
    for s in range(2):
        grad = (acc_dq[part(s), :] * (total[s, 0:1, :] * SCALE)).T.astype(BF16)
        for h in range(RATIO):
            dq_ref[run(s), h * DH : (h + 1) * DH] = grad[run(h)]
    second = end(b_moves, collect_b(at.zs - 1), zb_in)
    gk_ref[rows:, :] = second[:, :DH].astype(BF16)
    gv_ref[rows:, :] = second[:, DH:].astype(BF16)
    first = collect(last_a, keep.at[0], xa_in)
    gk_ref[:rows, :] = first[:, :DH].astype(BF16)
    gv_ref[:rows, :] = first[:, DH:].astype(BF16)
    for copy in sent:
        copy.wait_send()


def layer(x_count, positions, q_rows, k_rows, v_rows, dout):
    heads = lax.axis_size("head")
    rows = heads * q_rows.shape[0]
    width = q_rows.shape[1] // heads
    zs = 2 * (lax.axis_size("outer") // x_count)
    far = zs // 2
    run = rows // 2
    size = x_count * run
    batches = far + 2
    kv_width = 2 * DH
    dma = pltpu.SemaphoreType.DMA
    vmem = pl.BlockSpec(memory_space=pltpu.VMEM)
    sems = [(3, heads - 1), (3, heads - 1)]
    for x_dims, z_dims in (((x_count - 1,), (2, far, 2)), ((zs, 2), (2, far))) * 2:
        sems += [x_dims, x_dims, z_dims, z_dims, (zs,), (zs,)]
    sems[-4:-2] = [(2, far, 2)] * 2
    buffers = [
        ((rows, width), BF16),
        ((rows, kv_width), BF16),
        ((2, 2 * zs, size, kv_width), BF16),
        ((ROWS, 2 * DH), BF16),
        ((ROWS, 2 * DH), BF16),
        ((4, size, ROWS), F32),
        ((4, size, ROWS), F32),
        ((2 * zs, size, ROWS), BF16),
        ((2 * zs, size, ROWS), BF16),
        ((2, size, ROWS), BF16),
        ((2 * zs, size, kv_width), BF16),
        ((size, kv_width), BF16),
        ((2 * zs, kv_width, size), BF16),
        ((2 * zs, DH, size), BF16),
        ((2 * zs, size, ROWS), F32),
        ((2 * zs, size, ROWS), F32),
        ((4, kv_width, size), BF16),
        ((2, 8, ROWS), F32),
        ((2, 8, ROWS), F32),
        ((2, 8, ROWS), F32),
        ((batches, 2, 8, ROWS), F32),
        ((2 * DH, ROWS), F32),
        ((2 * DH, ROWS), F32),
        ((batches, ROWS, 2 * DH), BF16),
        ((batches, ROWS, 2 * DH), BF16),
        ((2, 8, ROWS), F32),
        ((2, 2, zs, size, kv_width), BF16),
        ((2, zs, size, kv_width), BF16),
        ((2, far, size, kv_width), BF16),
        ((2, far, size, kv_width), BF16),
        ((2, far, run, kv_width), BF16),
        ((2, far, run, kv_width), BF16),
        ((x_count - 1, run, kv_width), BF16),
        ((size, kv_width), BF16),
        ((zs, 3 * run, kv_width), BF16),
        ((zs, size, kv_width), BF16),
        ((zs, size, kv_width), F32),
    ]
    return pl.pallas_call(
        functools.partial(layer_kernel, x_count),
        out_shape=(jax.ShapeDtypeStruct((rows, width), BF16),) * 2
        + (jax.ShapeDtypeStruct((rows, DH), BF16),) * 2,
        in_specs=[pl.BlockSpec(memory_space=pltpu.SMEM)] + [vmem] * 4,
        out_specs=(vmem,) * 4,
        scratch_shapes=[pltpu.VMEM(dims, kind) for dims, kind in buffers]
        + [dma(dims) for dims in sems],
        compiler_params=pltpu.CompilerParams(
            collective_id=0, has_side_effects=True, vmem_limit_bytes=56 * 1024 * 1024
        ),
    )(positions, q_rows, k_rows, v_rows, dout)


def hand_in_kernel(*refs):
    half = len(refs) // 2
    for src, dst in zip(refs[:half], refs[half:]):
        dst[...] = src[...]


def hand_in(*results):
    vmem = pl.BlockSpec(memory_space=pltpu.VMEM)
    return pl.pallas_call(
        hand_in_kernel,
        out_shape=tuple(jax.ShapeDtypeStruct(x.shape, x.dtype) for x in results),
        in_specs=[vmem] * len(results),
        out_specs=(vmem,) * len(results),
    )(*results)


def shards(q_rows, k_rows, v_rows, dout, positions):
    return hand_in(*layer(CHIPS_X, positions, q_rows, k_rows, v_rows, dout))


def solution(mesh):
    return jax.shard_map(
        shards,
        mesh=mesh,
        in_specs=(
            P(("inner", "outer", "head"), None),
            P(("inner", "outer", "head"), None),
            P(("inner", "outer", "head"), None),
            P(("inner", "outer"), "head"),
            P(),
        ),
        out_specs=(
            P(("inner", "outer"), "head"),
            P(("inner", "outer"), "head"),
            P(("inner", "outer"), "head"),
            P(("inner", "outer"), "head"),
        ),
        check_vma=False,
    )
```

```python
import functools

import jax
import jax.numpy as jnp
from jax import lax
from jax.experimental import pallas as pl
from jax.experimental.pallas import tpu as pltpu
from jax.sharding import PartitionSpec as P

QH = 32
KVH = 8
DH = 128
RUN = 64
BLOCKS = 64
CHIPS_X = 4
RATIO = QH // KVH
ROWS = RATIO * RUN
CHUNK = 256
RUNS_CHUNK = CHUNK // RUN
CHUNKS = 2 * BLOCKS // RUNS_CHUNK
ITEMS = CHUNKS + 1
LOG2E = 1.4426950408889634
SCALE = DH**-0.5
NEG_FILL = -1e30
F32 = jnp.float32
BF16 = jnp.bfloat16


def dot(a, b, ca, cb):
    return lax.dot_general(a, b, (((ca,), (cb,)), ((), ())), preferred_element_type=F32)


MESH = pl.DeviceIdType.MESH


class Plane:
    def __init__(self, x_count):
        inner, outer = lax.axis_index("inner"), lax.axis_index("outer")
        self.xs = x_count
        self.z_pairs = lax.axis_size("outer") // x_count
        self.zs = 2 * self.z_pairs
        self.x = lax.rem(outer, x_count)
        self.core = lax.rem(inner, 2)
        self.z = 2 * lax.div(outer, x_count) + lax.div(inner, 2)

    def z_off(self, by):
        return lax.rem(self.z + by + self.zs, self.zs)

    def x_off(self, by):
        return lax.rem(self.x + by + self.xs, self.xs)

    def group(self, z, core):
        return (2 * lax.rem(z, 2) + core) * self.z_pairs + lax.div(z, 2)

    def device(self, z=None, core=None, x=None):
        z = self.z if z is None else z
        core = self.core if core is None else core
        x = self.x if x is None else x
        return {"inner": 2 * lax.rem(z, 2) + core, "outer": lax.div(z, 2) * self.xs + x}

    def partners(self):
        found = [self.device(core=1 - self.core)]
        found += [self.device(z=self.z_off(1)), self.device(z=self.z_off(-1))]
        found += [self.device(x=self.x_off(d)) for d in range(1, self.xs)]
        return found

    def greet(self, heads=1):
        head = lax.axis_index("head")
        partners = [{"head": lax.rem(head + d, heads)} for d in range(1, heads)]
        partners += self.partners()
        barrier = pltpu.get_barrier_semaphore()
        for device in partners:
            pl.semaphore_signal(barrier, inc=1, device_id=device, device_id_type=MESH)
        pl.semaphore_wait(barrier, len(partners))


def push(src, dst, send_sem, recv_sem, device):
    copy = pltpu.make_async_remote_copy(
        src_ref=src,
        dst_ref=dst,
        send_sem=send_sem,
        recv_sem=recv_sem,
        device_id=device,
        device_id_type=MESH,
    )
    copy.start()
    return copy


def layer_kernel(
    x_count,
    pos_ref,
    q_ref,
    k_ref,
    v_ref,
    do_ref,
    out_ref,
    dq_ref,
    gk_ref,
    gv_ref,
    q_got,
    block,
    kv,
    qs,
    dos,
    s_full,
    s_mix,
    e_full,
    e_mix,
    e_own,
    km,
    vm,
    km_t,
    ka_t,
    dp_full,
    dp_mix,
    vm_t,
    top,
    peak,
    total,
    marks,
    acc_out,
    acc_dq,
    qd,
    dod,
    delta,
    parts,
    other,
    za_in,
    za_out,
    zb_in,
    zb_out,
    xa_in,
    xa_out,
    xb_in,
    xb_out,
    keep,
    y_send,
    y_recv,
    *sems,
):
    at = Plane(x_count)
    heads = lax.axis_size("head")
    far = at.zs // 2
    tokens = q_ref.shape[0]
    width = q_ref.shape[1] // heads
    rows = block.shape[0] // 2
    size = x_count * rows
    ga, gb, sa, sb = (sems[6 * i : 6 * i + 6] for i in range(4))
    at.greet(heads)

    head = lax.axis_index("head")
    here = pl.ds(pl.multiple_of(head * tokens, tokens), tokens)
    q_moves, kv_moves = [], []
    for d in range(1, heads):
        peer = lax.rem(head + d, heads)
        cols = pl.ds(pl.multiple_of(peer * DH, DH), DH)
        for i, src in enumerate((k_ref, v_ref)):
            kv_moves.append(
                push(
                    src.at[:, cols],
                    block.at[here, pl.ds(i * DH, DH)],
                    y_send.at[i, d - 1],
                    y_recv.at[i, d - 1],
                    {"head": peer},
                )
            )
    for d in range(1, heads):
        peer = lax.rem(head + d, heads)
        cols = pl.ds(pl.multiple_of(peer * width, width), width)
        q_moves.append(
            push(
                q_ref.at[:, cols],
                q_got.at[here, :],
                y_send.at[2, d - 1],
                y_recv.at[2, d - 1],
                {"head": peer},
            )
        )
    cols = pl.ds(pl.multiple_of(head * DH, DH), DH)
    block[here, :DH] = k_ref[:, cols]
    block[here, DH:] = v_ref[:, cols]
    q_got[here, :] = q_ref[:, pl.ds(pl.multiple_of(head * width, width), width)]
    for copy in kv_moves:
        copy.wait_recv()
    sent = kv_moves + q_moves

    mine = pl.ds(pl.multiple_of(at.x * rows, rows), rows)
    own = at.group(at.z, at.core)
    kv[0, own, mine, :] = block[:rows, :]
    kv[1, own, mine, :] = block[rows:, :]

    def towards(way):
        return at.device(z=at.z_off(1 - 2 * way))

    def beside(src, dst, send, recv):
        copies = [
            push(src, dst, send.at[d - 1], recv.at[d - 1], at.device(x=at.x_off(d)))
            for d in range(1, at.xs)
        ]
        sent.extend(copies)
        return copies

    def arrive(copies):
        for copy in copies:
            copy.wait_recv()

    def move_a(way, step, group):
        part = kv.at[0, group]
        if step == far - 1:
            part = kv.at[0, group, pl.ds(way * (size // 2), size // 2), :]
        copy = push(part, part, ga[2].at[way, step], ga[3].at[way, step], towards(way))
        sent.append(copy)
        return copy

    def move_b(way, step, group):
        place = mine
        if step == far - 1:
            place = pl.ds(pl.multiple_of(at.x * rows + way * (rows // 2), rows // 2), rows // 2)
        part = kv.at[1, group, place, :]
        copy = push(part, part, gb[2].at[way, step], gb[3].at[way, step], towards(way))
        sent.append(copy)
        return copy

    crosses = {}

    def cross(half, i, group):
        whole = kv.at[half, group]
        send, recv = (gb, ga)[1 - half][4:]
        copy = push(whole, whole, send.at[i], recv.at[i], at.device(core=1 - at.core))
        sent.append(copy)
        crosses[half, i] = copy

    def spread(i, group):
        part = kv.at[1, group, mine, :]
        return i, group, beside(part, part, gb[0].at[i], gb[1].at[i])

    def finish(spreads):
        for i, group, copies in spreads:
            arrive(copies)
            cross(1, i, group)

    def fold(x, op):
        return op(x.reshape(x.shape[0] // 8, 8, ROWS), axis=0)

    def gap(group, r):
        mine_first = pos_ref[(x_count * own + at.x) * 2 * rows]
        return mine_first - pos_ref[(x_count * group + r) * 2 * rows]

    def early(group, r, shape=(RUN, ROWS)):
        return jnp.full(shape, gap(group, r), jnp.int32) >= 0

    def run(r):
        return slice(r * RUN, (r + 1) * RUN)

    def prepare(group):
        first, second = kv[0, group], kv[1, group]
        for r in range(x_count):
            is_early = early(group, r, (RUN, 2 * DH))
            left = jnp.where(is_early, first[run(r)].astype(F32), 0.0).astype(BF16)
            right = jnp.where(is_early, 0.0, second[run(r)].astype(F32)).astype(BF16)
            km[group, run(r), :] = jnp.concatenate([left[:, :DH], right[:, :DH]], axis=1)
            vm[run(r), :] = jnp.concatenate([left[:, DH:], right[:, DH:]], axis=1)
        km_t[group] = km[group].T
        ka_t[group] = first[:, :DH].T
        dp_full[group] = dot(first[:, DH:], dos[:, DH:], 1, 1)
        dp_mix[group] = dot(vm[...], dos[...], 1, 1)
        return vm[...].T

    def score(slot, group):
        full = dot(kv[0, group, :, :DH], qs[:, DH:], 1, 1)
        vm_t[slot] = prepare(group)
        mix = dot(km[group], qs[...], 1, 1)
        s_full[slot] = full
        s_mix[slot] = mix
        tops = [top[0], jnp.maximum(top[1], fold(full, jnp.max))]
        for r in range(x_count):
            is_early = early(group, r, (8, ROWS))
            highest = fold(mix[run(r)], jnp.max)
            tops[0] = jnp.maximum(tops[0], jnp.where(is_early, highest, NEG_FILL))
            tops[1] = jnp.maximum(tops[1], jnp.where(is_early, NEG_FILL, highest))
        top[0], top[1] = tops

    def score_own():
        first, second = kv[0, own, :, :DH], kv[1, own, :, :DH]
        full = dot(first, qs[:, DH:], 1, 1)
        one = dot(first, qs[:, :DH], 1, 1)
        two = dot(second, qs[:, DH:], 1, 1)
        s_full[0] = full
        key = lax.broadcasted_iota(jnp.int32, (RUN, ROWS), 0)
        row = lax.rem(lax.broadcasted_iota(jnp.int32, (RUN, ROWS), 1), RUN)
        tops = [top[0], jnp.maximum(top[1], fold(full, jnp.max))]
        for r in range(x_count):
            away = gap(own, r)
            for s, (tile, sign) in enumerate(((one, 1), (two, -1))):
                masked = jnp.where(key - row <= sign * away, tile[run(r)], NEG_FILL)
                s_mix[s, run(r), :] = masked
                tops[s] = jnp.maximum(tops[s], fold(masked, jnp.max))
        top[0], top[1] = tops

    def part(s):
        return slice(s * DH, (s + 1) * DH)

    def renew(batch):
        for s in range(2):
            highest = jnp.max(top[s], axis=0, keepdims=True)
            factor = jnp.exp2((peak[s, 0:1, :] - highest) * (SCALE * LOG2E))
            total[s] = total[s] * factor
            acc_out[part(s), :] = acc_out[part(s), :] * factor
            peak[s] = jnp.broadcast_to(highest, (8, ROWS))
            marks[batch, s] = jnp.broadcast_to(highest, (8, ROWS))

    def weigh(slot, group):
        highs = [peak[s] * (SCALE * LOG2E) for s in range(2)]
        full = jnp.exp2(s_full[slot] * (SCALE * LOG2E) - highs[1][0:1])
        totals = [total[0], total[1] + fold(full, jnp.sum)]
        full = full.astype(BF16)
        e_full[group] = full
        for r in range(x_count):
            is_early = early(group, r, (8, ROWS))
            high = jnp.where(is_early, highs[0], highs[1])[0:1]
            e = jnp.exp2(s_mix[slot, run(r), :] * (SCALE * LOG2E) - high)
            e_mix[group, run(r), :] = e.astype(BF16)
            summed = fold(e, jnp.sum)
            totals[0] = totals[0] + jnp.where(is_early, summed, 0.0)
            totals[1] = totals[1] + jnp.where(is_early, 0.0, summed)
        total[0], total[1] = totals
        acc_out[...] = acc_out[...] + dot(vm_t[slot], e_mix[group], 1, 0)
        acc_out[DH:, :] = acc_out[DH:, :] + dot(kv[0, group, :, DH:].T, full, 1, 0)

    def weigh_own():
        full = jnp.exp2((s_full[0] - peak[1, 0:1, :]) * (SCALE * LOG2E))
        one = jnp.exp2((s_mix[0] - peak[0, 0:1, :]) * (SCALE * LOG2E))
        two = jnp.exp2((s_mix[1] - peak[1, 0:1, :]) * (SCALE * LOG2E))
        total[0] = total[0] + fold(one, jnp.sum)
        total[1] = total[1] + fold(full, jnp.sum) + fold(two, jnp.sum)
        e_full[own] = full.astype(BF16)
        e_own[0] = one.astype(BF16)
        e_own[1] = two.astype(BF16)
        first, second = kv[0, own, :, DH:].T, kv[1, own, :, DH:].T
        acc_out[:DH, :] = acc_out[:DH, :] + dot(first, e_own[0], 1, 0)
        acc_out[DH:, :] = (
            acc_out[DH:, :] + dot(first, e_full[own], 1, 0) + dot(second, e_own[1], 1, 0)
        )

    def forward(batch, count, group_of):
        def first(j, carry):
            score(j, group_of(j))
            return carry

        def then(j, carry):
            weigh(j, group_of(j))
            return carry

        lax.fori_loop(0, count, first, 0)
        renew(batch)
        lax.fori_loop(0, count, then, 0)

    a_first = beside(kv.at[0, own, mine, :], kv.at[0, own, mine, :], ga[0], ga[1])
    b_moves = [move_b(way, 0, own) for way in range(2)]
    spreads = [spread(0, own)]
    arrive(a_first)
    a_moves = [move_a(way, 0, own) for way in range(2)]
    cross(0, 0, own)
    arrive(q_moves)
    for s in range(2):
        for h in range(RATIO):
            cols = slice(h * DH, (h + 1) * DH)
            qs[run(h), part(s)] = q_got[run(s), cols]
            dos[run(h), part(s)] = do_ref[run(s), cols]
    top[...] = jnp.full(top.shape, NEG_FILL, F32)
    peak[...] = jnp.full(peak.shape, NEG_FILL, F32)
    total[...] = jnp.zeros(total.shape, F32)
    acc_out[...] = jnp.zeros(acc_out.shape, F32)
    acc_dq[...] = jnp.zeros(acc_dq.shape, F32)
    finish(spreads)
    score_own()
    renew(0)
    weigh_own()

    def both(by):
        return lambda j: at.group(
            at.z_off(by * (2 * lax.rem(j, 2) - 1)), lax.rem(at.core + lax.div(j, 2), 2)
        )

    def crossed(indices):
        for i in indices:
            for half in range(2):
                crosses[half, i].wait_recv()

    for step in range(far):
        groups = [at.group(at.z_off((2 * way - 1) * (step + 1)), at.core) for way in range(2)]
        last = step == far - 1
        if last:
            arrive(b_moves)
            spreads = [spread(2 * far - 1, groups[0])]
            arrive(a_moves)
            cross(0, 2 * far - 1, groups[0])
        else:
            for way in range(2):
                a_moves[way].wait_recv()
                a_moves[way] = move_a(way, step + 1, groups[way])
            arrive(b_moves)
            b_moves = [move_b(way, step + 1, groups[way]) for way in range(2)]
            spreads = [spread(2 * step + 1 + way, groups[way]) for way in range(2)]
            for way in range(2):
                cross(0, 2 * step + 1 + way, groups[way])
        if step == 0:
            crossed([0])
            forward(1, 1, lambda j: at.group(at.z, 1 - at.core))
        else:
            crossed([2 * step - 1, 2 * step])
            forward(1 + step, 4, both(step))
        finish(spreads)
    farthest = [at.group(at.z_off(far), core) for core in (at.core, 1 - at.core)]
    score(0, farthest[0])
    crossed([2 * far - 1])
    score(1, farthest[1])
    renew(1 + far)
    for j in range(2):
        weigh(j, farthest[j])

    def output(s):
        return (acc_out[part(s), :] * total[s, 0:1, :]).astype(BF16).astype(F32)

    def emit_output():
        for s in range(2):
            out = output(s).T.astype(BF16)
            for h in range(RATIO):
                out_ref[run(s), h * DH : (h + 1) * DH] = out[run(h)]

    def scale(batch):
        for s in range(2):
            factor = jnp.exp2((marks[batch, s] - peak[s]) * (SCALE * LOG2E))
            marks[batch, s] = factor
            by_row = jnp.broadcast_to(factor[0:1] * total[s, 0:1, :], (DH, ROWS)).T
            dod[batch, :, part(s)] = (dos[:, part(s)].astype(F32) * by_row).astype(BF16)
            qd[batch, :, part(s)] = (qs[:, part(s)].astype(F32) * (by_row * SCALE)).astype(BF16)

    for s in range(2):
        inv = 1.0 / jnp.sum(total[s], axis=0, keepdims=True)
        total[s] = jnp.broadcast_to(inv, (8, ROWS))
        d_rows = dos[:, part(s)].astype(F32)
        delta[s] = jnp.broadcast_to(jnp.sum(output(s) * d_rows.T, axis=0, keepdims=True), (8, ROWS))
    scale(1 + far)

    def backward(group, batch, who, i):
        full, mix = e_full[group], e_mix[group]
        ds_full = (full.astype(F32) * (dp_full[group] - delta[1, 0:1, :])).astype(BF16)
        ds_mix = []
        for r in range(x_count):
            shift = jnp.where(early(group, r, (8, ROWS)), delta[0], delta[1])[0:1]
            e = e_mix[group, run(r), :].astype(F32)
            ds_mix.append((e * (dp_mix[group, run(r), :] - shift)).astype(BF16))
        ds_mix = jnp.concatenate(ds_mix, axis=0)
        for cols, left, right, scaled in (
            (slice(0, DH), ds_full, ds_mix, qd),
            (slice(DH, 2 * DH), full, mix, dod),
        ):
            whole = dot(left, scaled[batch, :, DH:], 1, 0)
            mixed = dot(right, scaled[batch], 1, 0)
            for r in range(x_count):
                is_early = early(group, r, (RUN, DH))
                first = whole[run(r)] + jnp.where(is_early, mixed[run(r), :DH], 0.0)
                second = jnp.where(is_early, 0.0, mixed[run(r), DH:])
                parts[who, 0, i, run(r), cols] = first.astype(BF16)
                parts[who, 1, i, run(r), cols] = second.astype(BF16)
        grad = dot(km_t[group], ds_mix, 1, 0)
        late = grad[DH:] + dot(ka_t[group], ds_full, 1, 0)
        acc_dq[:DH, :] = acc_dq[:DH, :] + marks[batch, 0, 0:1, :] * grad[:DH]
        acc_dq[DH:, :] = acc_dq[DH:, :] + marks[batch, 1, 0:1, :] * late

    def backward_own(i):
        first, second = kv[0, own], kv[1, own]
        d_one, d_two = delta[0, 0:1, :], delta[1, 0:1, :]

        def ds(e, values, s, shift):
            dp = dot(values[:, DH:], dos[:, part(s)], 1, 1)
            return (e.astype(F32) * (dp - shift)).astype(BF16)

        ds_full = ds(e_full[own], first, 1, d_two)
        ds_one = ds(e_own[0], first, 0, d_one)
        ds_two = ds(e_own[1], second, 1, d_two)
        for cols, full, one, two, scaled in (
            (slice(0, DH), ds_full, ds_one, ds_two, qd),
            (slice(DH, 2 * DH), e_full[own], e_own[0], e_own[1], dod),
        ):
            parts[1, 0, i, :, cols] = (
                dot(full, scaled[0, :, DH:], 1, 0) + dot(one, scaled[0, :, :DH], 1, 0)
            ).astype(BF16)
            parts[1, 1, i, :, cols] = dot(two, scaled[0, :, DH:], 1, 0).astype(BF16)
        first, second = first[:, :DH].T, second[:, :DH].T
        acc_dq[:DH, :] = acc_dq[:DH, :] + marks[0, 0, 0:1, :] * dot(first, ds_one, 1, 0)
        acc_dq[DH:, :] = acc_dq[DH:, :] + marks[0, 1, 0:1, :] * (
            dot(first, ds_full, 1, 0) + dot(second, ds_two, 1, 0)
        )

    hand_over = {}

    def give(i):
        for half in (1, 0):
            send, recv = (sb, sa)[1 - half][4:]
            copy = push(
                parts.at[0, half, i],
                other.at[half, i],
                send.at[i],
                recv.at[i],
                at.device(core=1 - at.core),
            )
            sent.append(copy)
            hand_over[half, i] = copy

    def pair(half, i):
        hand_over[half, i].wait_recv()
        return parts[1, half, i].astype(F32) + other[half, i].astype(F32)

    def across(src, dst, send, recv):
        copies = []
        for d in range(1, at.xs):
            x = at.x_off(d)
            place = pl.ds(pl.multiple_of(x * rows, rows), rows)
            copies.append(
                push(src.at[place, :], dst.at[d - 1], send.at[d - 1], recv.at[d - 1], at.device(x=x))
            )
        sent.extend(copies)
        return copies

    def spread_b(i):
        both_cores = pair(1, i)
        keep[i] = both_cores
        xb_out[i] = both_cores.astype(BF16)
        return across(xb_out.at[i], xb_in.at[i], sb[0].at[i], sb[1].at[i])

    def collect(copies, kept, arrived):
        summed = kept[mine, :]
        for d in range(1, at.xs):
            copies[d - 1].wait_recv()
            summed = summed + arrived[d - 1].astype(F32)
        return summed

    def collect_b(i):
        return collect(b_spreads[i], keep.at[i], xb_in.at[i])

    def half_of(way, length):
        return slice(way * (length // 2), (way + 1) * (length // 2))

    def along(out, into, sems, way, step):
        length = out.shape[2]
        place = pl.ds(way * (length // 2), length // 2) if step == 0 else pl.ds(0, length)
        copy = push(
            out.at[way, step, place, :],
            into.at[way, step, place, :],
            sems[2].at[way, step],
            sems[3].at[way, step],
            towards(way),
        )
        sent.append(copy)
        return copy

    def begin(summed, out, into, sems):
        moves = []
        for way in range(2):
            place = half_of(way, out.shape[2])
            out[way, 0, place, :] = summed[place].astype(BF16)
            moves.append(along(out, into, sems, way, 0))
        return moves

    def go_on(moves, way, step, summed, out, into, sems):
        moves[way].wait_recv()
        if step == 1:
            near, rest = half_of(way, out.shape[2]), half_of(1 - way, out.shape[2])
            out[way, 1, near, :] = (summed[near] + into[way, 0, near, :].astype(F32)).astype(BF16)
            out[way, 1, rest, :] = summed[rest].astype(BF16)
        else:
            out[way, step] = (summed + into[way, step - 1].astype(F32)).astype(BF16)
        moves[way] = along(out, into, sems, way, step)

    def end(moves, summed, into):
        for way in range(2):
            moves[way].wait_recv()
            summed = summed + into[way, far - 1].astype(F32)
        return summed

    def back(who, step):
        core = lax.rem(at.core + 1 + who, 2)

        def one_way(way, carry):
            offset = (far - step) * (1 - 2 * way)
            group = at.group(at.z_off(offset), core)
            backward(group, 1 + far - step, who, 2 * step - 1 + way)
            return carry

        lax.fori_loop(0, 2, one_way, 0)

    a_refs = (za_out, za_in, sa)
    b_refs = (zb_out, zb_in, sb)
    backward(at.group(at.z_off(far), 1 - at.core), 1 + far, 0, 0)
    give(0)
    backward(at.group(at.z_off(far), at.core), 1 + far, 1, 0)
    b_spreads = {0: spread_b(0)}
    a_moves = begin(pair(0, 0), *a_refs)
    for batch in range(1 + far):
        scale(batch)
    emit_output()
    b_moves = None
    for step in range(1, far):
        back(0, step)
        give(2 * step - 1)
        give(2 * step)
        back(1, step)
        for way in range(2):
            b_spreads[2 * step - 1 + way] = spread_b(2 * step - 1 + way)
        for way in range(2):
            go_on(a_moves, way, step, pair(0, 2 * step - 1 + way), *a_refs)
        if step == 1:
            b_moves = begin(collect_b(0), *b_refs)
        else:
            for way in range(2):
                go_on(b_moves, way, step - 1, collect_b(2 * step - 3 + way), *b_refs)
    backward(at.group(at.z, 1 - at.core), 1, 0, at.zs - 1)
    give(at.zs - 1)
    for way in range(2):
        go_on(b_moves, way, far - 1, collect_b(2 * far - 3 + way), *b_refs)
    backward_own(at.zs - 1)
    b_spreads[at.zs - 1] = spread_b(at.zs - 1)
    mine_a = end(a_moves, pair(0, at.zs - 1), za_in)
    other_a = keep.at[0]
    other_a[...] = mine_a
    xa_out[...] = mine_a.astype(BF16)
    last_a = across(xa_out, xa_in, sa[0], sa[1])
    for s in range(2):
        grad = (acc_dq[part(s), :] * (total[s, 0:1, :] * SCALE)).T.astype(BF16)
        for h in range(RATIO):
            dq_ref[run(s), h * DH : (h + 1) * DH] = grad[run(h)]
    second = end(b_moves, collect_b(at.zs - 1), zb_in)
    gk_ref[rows:, :] = second[:, :DH].astype(BF16)
    gv_ref[rows:, :] = second[:, DH:].astype(BF16)
    first = collect(last_a, keep.at[0], xa_in)
    gk_ref[:rows, :] = first[:, :DH].astype(BF16)
    gv_ref[:rows, :] = first[:, DH:].astype(BF16)
    for copy in sent:
        copy.wait_send()


def layer(x_count, positions, q_rows, k_rows, v_rows, dout):
    heads = lax.axis_size("head")
    rows = heads * q_rows.shape[0]
    width = q_rows.shape[1] // heads
    zs = 2 * (lax.axis_size("outer") // x_count)
    far = zs // 2
    run = rows // 2
    size = x_count * run
    batches = far + 2
    kv_width = 2 * DH
    dma = pltpu.SemaphoreType.DMA
    vmem = pl.BlockSpec(memory_space=pltpu.VMEM)
    sems = [(3, heads - 1), (3, heads - 1)]
    for x_dims in ((x_count - 1,), (zs, x_count - 1)) * 2:
        sems += [x_dims, x_dims, (2, far), (2, far), (zs,), (zs,)]
    buffers = [
        ((rows, width), BF16),
        ((rows, kv_width), BF16),
        ((2, 2 * zs, size, kv_width), BF16),
        ((ROWS, 2 * DH), BF16),
        ((ROWS, 2 * DH), BF16),
        ((4, size, ROWS), F32),
        ((4, size, ROWS), F32),
        ((2 * zs, size, ROWS), BF16),
        ((2 * zs, size, ROWS), BF16),
        ((2, size, ROWS), BF16),
        ((2 * zs, size, kv_width), BF16),
        ((size, kv_width), BF16),
        ((2 * zs, kv_width, size), BF16),
        ((2 * zs, DH, size), BF16),
        ((2 * zs, size, ROWS), F32),
        ((2 * zs, size, ROWS), F32),
        ((4, kv_width, size), BF16),
        ((2, 8, ROWS), F32),
        ((2, 8, ROWS), F32),
        ((2, 8, ROWS), F32),
        ((batches, 2, 8, ROWS), F32),
        ((2 * DH, ROWS), F32),
        ((2 * DH, ROWS), F32),
        ((batches, ROWS, 2 * DH), BF16),
        ((batches, ROWS, 2 * DH), BF16),
        ((2, 8, ROWS), F32),
        ((2, 2, zs, size, kv_width), BF16),
        ((2, zs, size, kv_width), BF16),
        ((2, far, size, kv_width), BF16),
        ((2, far, size, kv_width), BF16),
        ((2, far, run, kv_width), BF16),
        ((2, far, run, kv_width), BF16),
        ((x_count - 1, run, kv_width), BF16),
        ((size, kv_width), BF16),
        ((zs, x_count - 1, run, kv_width), BF16),
        ((zs, size, kv_width), BF16),
        ((zs, size, kv_width), F32),
    ]
    return pl.pallas_call(
        functools.partial(layer_kernel, x_count),
        out_shape=(jax.ShapeDtypeStruct((rows, width), BF16),) * 2
        + (jax.ShapeDtypeStruct((rows, DH), BF16),) * 2,
        in_specs=[pl.BlockSpec(memory_space=pltpu.SMEM)] + [vmem] * 4,
        out_specs=(vmem,) * 4,
        scratch_shapes=[pltpu.VMEM(dims, kind) for dims, kind in buffers]
        + [dma(dims) for dims in sems],
        compiler_params=pltpu.CompilerParams(
            collective_id=0, has_side_effects=True, vmem_limit_bytes=56 * 1024 * 1024
        ),
    )(positions, q_rows, k_rows, v_rows, dout)


def hand_in_kernel(*refs):
    half = len(refs) // 2
    for src, dst in zip(refs[:half], refs[half:]):
        dst[...] = src[...]


def hand_in(*results):
    vmem = pl.BlockSpec(memory_space=pltpu.VMEM)
    return pl.pallas_call(
        hand_in_kernel,
        out_shape=tuple(jax.ShapeDtypeStruct(x.shape, x.dtype) for x in results),
        in_specs=[vmem] * len(results),
        out_specs=(vmem,) * len(results),
    )(*results)


def shards(q_rows, k_rows, v_rows, dout, positions):
    return hand_in(*layer(CHIPS_X, positions, q_rows, k_rows, v_rows, dout))


def solution(mesh):
    return jax.shard_map(
        shards,
        mesh=mesh,
        in_specs=(
            P(("inner", "outer", "head"), None),
            P(("inner", "outer", "head"), None),
            P(("inner", "outer", "head"), None),
            P(("inner", "outer"), "head"),
            P(),
        ),
        out_specs=(
            P(("inner", "outer"), "head"),
            P(("inner", "outer"), "head"),
            P(("inner", "outer"), "head"),
            P(("inner", "outer"), "head"),
        ),
        check_vma=False,
    )
```
